32 devices in a mesh: dp: 4 (over y, core), seq: 8 (over z, x).
Axes of the slice: x: 2, y: 2, z: 4, core: 2. Of those that a mesh axis runs over, the one named last changes fastest.
Arguments:
- tokens: bfloat16 [4, 8192, 1152], P('dp', 'seq'), may hold values from -6 to 6
- segments: int32 [4, 8192], P('dp', 'seq'), may hold values from 0 to 63, as said below
- condition: bfloat16 [4, 64, 1152], P('dp'), may hold values from -6 to 6
- cotangent: bfloat16 [4, 8192, 1152], P('dp', 'seq'), may hold values from -6 to 6
- modulation_weight: bfloat16 [1152, 6912], P('dp'), may hold values from -0.1875 to 0.1875
- modulation_bias: bfloat16 [6912], replicated, may hold values from -1.796875 to 1.796875
- input_weight: bfloat16 [1152, 3456], P('dp'), may hold values from -0.1875 to 0.1875
- query_value_bias: bfloat16 [2304], replicated, may hold values from -1.796875 to 1.796875
- output_weight: bfloat16 [1152, 1152], P('dp'), may hold values from -2 to 2
- output_bias: bfloat16 [1152], replicated, may hold values from -1.796875 to 1.796875
- expand_weight: bfloat16 [1152, 4608], P('dp'), may hold values from -0.1875 to 0.1875
- expand_bias: bfloat16 [4608], replicated, may hold values from -1.796875 to 1.796875
- contract_weight: bfloat16 [4608, 1152], P('dp'), may hold values from -0.09375 to 0.09375
- contract_bias: bfloat16 [1152], replicated, may hold values from -1.796875 to 1.796875
Outputs:
- layer_out: bfloat16 [4, 8192, 1152], P('dp', 'seq')
- grad_tokens: float32 [4, 8192, 1152], P('dp', 'seq')
- grad_condition: float32 [4, 64, 1152], P('dp', 'seq')
- grad_modulation_weight: float32 [1152, 6912], P('dp', 'seq')
- grad_modulation_bias: float32 [6912], replicated
- grad_input_weight: float32 [1152, 3456], P('dp', 'seq')
- grad_query_value_bias: float32 [2304], replicated
- grad_output_weight: float32 [1152, 1152], P('dp', 'seq')
- grad_output_bias: float32 [1152], replicated
- grad_expand_weight: float32 [1152, 4608], P('dp', 'seq')
- grad_expand_bias: float32 [4608], replicated
- grad_contract_weight: float32 [4608, 1152], P('dp', 'seq')
- grad_contract_bias: float32 [1152], replicated
The draws below stay inside these ranges and needn't reach their ends.
Inputs may be any that keep to these rules, and one draw needn't show every extreme that they name: `segments`: in each group the rows run through images 0 to 63 in order, each image one contiguous run of 64 to 192 rows; in every group some image has exactly 192 rows.
All inputs are finite; a program needn't handle non-finite values.
Results may differ from the reference program's by a relative error of at most 0.012.
The reference program's roundings to bfloat16 on the way count: a program that leaves them out, or rounds other values in their place, can miss the bound.
Values may be sent and summed in bfloat16 or wider, within the bound.
No kernel may reach another device: no remote copies, remote signals or barrier semaphores. Data moves between devices by JAX's collectives and lax.ppermute only.
A program may use at most 448 MiB of HBM per device.

```python
import math
from functools import partial
import jax
import jax.numpy as jnp
from jax import lax

D = 1152
HEADS = 16
HEAD_DIM = 72
FF = 4608
TOK_DEV = 1024
MINLEN = 64
MAXLEN = 192
IMG_DEV = 8
IMAGES = 64
ROWS = 8192
GROUPS = 4
N_DP = 4
N_SEQ = 8


def draw_segments(key, part):
    key = jax.random.fold_in(key, 11)
    spread = MAXLEN - MINLEN
    pair_count = IMG_DEV * N_SEQ // 2

    def one_group(group_key):
        first_key, order_key = jax.random.split(group_key)
        extra_rows = jax.random.randint(first_key, (pair_count,), 0, spread + 1).astype(jnp.int32)
        extra_rows = extra_rows.at[0].set(spread)
        lengths = MINLEN + jnp.concatenate([extra_rows, spread - extra_rows])
        lengths = lengths[jax.random.permutation(order_key, 2 * pair_count)]
        boundary = jnp.cumsum(lengths).astype(jnp.int32)
        positions = jnp.arange(TOK_DEV * N_SEQ, dtype=jnp.int32)
        return jnp.searchsorted(boundary, positions, side='right').astype(jnp.int32)
    group_keys = jax.random.split(key, N_DP)
    return jax.vmap(one_group)(group_keys)


def steps_of(key, shape, cuts, smallest, high):
    factor_of, own = 1.0, jax.random.fold_in(key, 6)
    for dim, parts in cuts:
        steps = jnp.exp(jax.random.uniform(jax.random.fold_in(own, dim), (parts,), jnp.float32, smallest / len(cuts), high / len(cuts)))
        factor_of = factor_of * jnp.repeat(steps, shape[dim] // parts).reshape([-1 if axis == dim else 1 for axis in range(len(shape))])
    return factor_of


def bell_draw(rng, dims, scale, reach, cuts=(), kind=jnp.bfloat16):
    factor_of = steps_of(rng, dims, cuts, -0.22, 0.18) if cuts else 1.0
    values = jax.random.normal(rng, dims, jnp.float32) * scale * factor_of
    return jnp.minimum(jnp.maximum(values, -reach), reach).astype(kind)


def setup_inputs(seed: int = 0) -> dict:
    splits = jax.random.split(jax.random.key(seed), 15)
    tokens = bell_draw(splits[0], (GROUPS, ROWS, D), 1.0, 6.0, ((0, 4), (1, 8)))
    segments = draw_segments(jax.random.fold_in(splits[14], 71), 0)
    condition = bell_draw(splits[2], (GROUPS, IMAGES, D), 1.0, 6.0, ((0, 4),))
    cotangent = bell_draw(splits[3], (GROUPS, ROWS, D), 1.0, 6.0, ((0, 4), (1, 8)))
    modulation_weight = bell_draw(splits[4], (D, 6 * D), D ** -0.5, 0.1875, ((0, 4),))
    modulation_bias = bell_draw(splits[5], (6 * D,), 0.3, 1.796875)
    input_weight = bell_draw(splits[6], (D, 3 * D), D ** -0.5, 0.1875, ((0, 4),))
    query_value_bias = bell_draw(splits[7], (2 * D,), 0.3, 1.796875)
    output_weight = bell_draw(splits[8], (D, D), (max(2 * D // (MINLEN + MAXLEN), 4)) ** -0.5, 2.0, ((0, 4),))
    output_bias = bell_draw(splits[9], (D,), 0.3, 1.796875)
    expand_weight = bell_draw(splits[10], (D, FF), D ** -0.5, 0.1875, ((0, 4),))
    expand_bias = bell_draw(splits[11], (FF,), 0.3, 1.796875)
    contract_weight = bell_draw(splits[12], (FF, D), FF ** -0.5, 0.09375, ((0, 4),))
    contract_bias = bell_draw(splits[13], (D,), 0.3, 1.796875)
    return {"tokens": tokens, "segments": segments, "condition": condition, "cotangent": cotangent, "modulation_weight": modulation_weight, "modulation_bias": modulation_bias, "input_weight": input_weight, "query_value_bias": query_value_bias, "output_weight": output_weight, "output_bias": output_bias, "expand_weight": expand_weight, "expand_bias": expand_bias, "contract_weight": contract_weight, "contract_bias": contract_bias}


@jax.custom_vjp
def low(v):
    return lax.optimization_barrier(v.astype(jnp.bfloat16)).astype(jnp.float32)

@jax.custom_vjp
def low_back(v):
    return v

def low_keep(v):
    return (low(v), None)

def low_pass(kept, grad):
    return (grad,)

def back_keep(v):
    return (v, None)

def back_low(kept, grad):
    return (low(grad),)
low.defvjp(low_keep, low_pass)
low_back.defvjp(back_keep, back_low)
epsilon = 1e-06
highest = lax.Precision.HIGHEST

def matmul_high(operand, matrix):
    return jnp.dot(operand, matrix, precision=highest)

def layer_norm(token_rows):
    centred = token_rows - lax.optimization_barrier(jnp.mean(token_rows, axis=-1, keepdims=True))
    return centred * lax.rsqrt(lax.optimization_barrier(jnp.mean(centred * centred, axis=-1, keepdims=True)) + epsilon)

def attention(queries, key_rows, values, segment):
    row_count = queries.shape[0]
    block_rows = min(512, TOK_DEV)
    window_rows = block_rows + 2 * MAXLEN
    score_scale = 1.0 / math.sqrt(HEAD_DIM)
    marker = segment + 1
    padded_pairs = jnp.pad(jnp.concatenate([key_rows, values], axis=1), ((MAXLEN, MAXLEN), (0, 0)))
    padded_marker = jnp.pad(marker, (MAXLEN, MAXLEN))

    def one_block(block_index):
        block_start = block_index * block_rows
        query_block = lax.dynamic_slice_in_dim(queries, block_start, block_rows, 0).reshape(block_rows, HEADS, HEAD_DIM)
        own_marker = lax.dynamic_slice_in_dim(marker, block_start, block_rows, 0)
        pair_window = lax.dynamic_slice_in_dim(padded_pairs, block_start, window_rows, 0)
        mark_window = lax.dynamic_slice_in_dim(padded_marker, block_start, window_rows, 0)
        key_block = pair_window[:, :D].reshape(window_rows, HEADS, HEAD_DIM)
        value_block = pair_window[:, D:].reshape(window_rows, HEADS, HEAD_DIM)
        raw_scores = low_back(jnp.einsum('qhd,khd->hqk', query_block, key_block, precision=highest) * score_scale)
        matching = (own_marker[:, None] == mark_window[None, :])[None]
        masked = jnp.where(matching, raw_scores, -1e+30)
        exponent = jnp.exp(masked - lax.optimization_barrier(jnp.max(masked, axis=-1, keepdims=True)))
        probability = low(exponent / lax.optimization_barrier(jnp.sum(exponent, axis=-1, keepdims=True)))
        return jnp.einsum('hqk,khd->qhd', probability, value_block, precision=highest).reshape(block_rows, D)
    blocks = lax.map(jax.checkpoint(one_block), jnp.arange(row_count // block_rows, dtype=jnp.int32))
    return blocks.reshape(row_count, D)

def forward_group(tokens, condition, modulation_weight, modulation_bias, input_weight, query_value_bias, output_weight, output_bias, expand_weight, expand_bias, contract_weight, contract_bias, segment=None):
    modulation = matmul_high(low(jax.nn.silu(condition)), modulation_weight) + modulation_bias
    per_row = jnp.take(modulation, segment, axis=0)
    shift_mixer, scale_mixer, gate_mixer, shift_feed, scale_feed, gate_feed = jnp.split(per_row, 6, axis=1)
    input_attn = low(layer_norm(tokens) * (1.0 + scale_mixer) + shift_mixer)
    packed = matmul_high(input_attn, input_weight)
    queries = low(low_back(packed[:, :D] + query_value_bias[:D]))
    key_rows = low(low_back(packed[:, D:2 * D]))
    values = low(low_back(packed[:, 2 * D:] + query_value_bias[D:]))
    attn_mixed = low(low_back(attention(queries, key_rows, values, segment)))
    attn_out = low_back(matmul_high(attn_mixed, output_weight) + output_bias)
    middle = tokens + gate_mixer * attn_out
    input_feed = low(layer_norm(middle) * (1.0 + scale_feed) + shift_feed)
    hidden = low_back(matmul_high(input_feed, expand_weight) + expand_bias)
    active = low(jax.nn.gelu(hidden, approximate=True))
    feed_out = low_back(matmul_high(active, contract_weight) + contract_bias)
    return middle + gate_feed * feed_out

def reference(tokens, segments, condition, cotangent, modulation_weight, modulation_bias, input_weight, query_value_bias, output_weight, output_bias, expand_weight, expand_bias, contract_weight, contract_bias):
    weights = tuple((argument.astype(jnp.float32) for argument in (modulation_weight, modulation_bias, input_weight, query_value_bias, output_weight, output_bias, expand_weight, expand_bias, contract_weight, contract_bias)))
    layer_outs = []
    token_grads = []
    cond_grads = []
    weight_grads = None
    for group_index in range(tokens.shape[0]):
        function = partial(forward_group, segment=segments[group_index])
        layer_value, pullback = jax.vjp(function, tokens[group_index].astype(jnp.float32), condition[group_index].astype(jnp.float32), *weights)
        gradients = pullback(cotangent[group_index].astype(jnp.float32))
        layer_outs.append(layer_value.astype(jnp.bfloat16))
        token_grads.append(gradients[0])
        cond_grads.append(gradients[1])
        if weight_grads is None:
            weight_grads = tuple(gradients[2:])
        else:
            weight_grads = jax.tree.map(jnp.add, weight_grads, tuple(gradients[2:]))
    return (jnp.stack(layer_outs), jnp.stack(token_grads), jnp.stack(cond_grads), weight_grads[0], weight_grads[1], weight_grads[2], weight_grads[3], weight_grads[4], weight_grads[5], weight_grads[6], weight_grads[7], weight_grads[8], weight_grads[9])
```

```python
import functools
from functools import partial
import math

import jax
import jax.numpy as jnp
from jax import lax
from jax.experimental import pallas as pl
from jax.experimental.pallas import tpu as pltpu
from jax.sharding import PartitionSpec as P

WIN = 18
HEADS = 16
MAXLEN = 192
HEAD = 72
BLOCK = 256
SPAN = BLOCK + 2 * MAXLEN
CHUNK = 128
BF, F32 = jnp.bfloat16, jnp.float32
SCORE_SCALE = 1.0 / math.sqrt(HEAD)
LOG2E = 1.4426950408889634
VMEM = 60 * 1024 * 1024


def dot_rows(left, right):
    return lax.dot_general(left, right, (((1,), (1,)), ((), ())), preferred_element_type=F32)


def dot_plain(left, right):
    return jnp.dot(left, right, preferred_element_type=F32)


def fill_mask(key_mark_ref, query_mark_ref, bias):
    marks = jnp.broadcast_to(key_mark_ref[0].astype(F32), (CHUNK, SPAN))
    columns = marks.T
    query = query_mark_ref[0].astype(F32)
    for lane in range(0, BLOCK, CHUNK):
        bias[:, lane : lane + CHUNK] = jnp.where(
            columns == query[:, lane : lane + CHUNK], 0.0, -1e30
        )


def head_lanes(head, width):
    first = jnp.minimum((head * HEAD) // 128 * 128, width - 256)
    lanes = lax.broadcasted_iota(jnp.int32, (1, 256), 1) + first
    inside = (lanes >= head * HEAD) & (lanes < (head + 1) * HEAD)
    return pl.multiple_of(first, 128), inside


def masked(ref, first, inside):
    block = ref[:, pl.ds(first, 256)]
    return jnp.where(inside, block, jnp.zeros_like(block))


def take_window(edge, step, prev_ref, own_ref, next_ref, window):
    rows = own_ref.shape[0]
    inner = SPAN - MAXLEN
    if not edge:
        return own_ref.at[pl.ds(pl.multiple_of(step * BLOCK + BLOCK - MAXLEN, 64), SPAN)]

    @pl.when(step == 0)
    def _():
        window[0:MAXLEN, :] = prev_ref[...]
        window[MAXLEN:SPAN, :] = own_ref[0:inner, :]

    @pl.when(step == 1)
    def _():
        window[0:inner, :] = own_ref[rows - inner : rows, :]
        window[inner:SPAN, :] = next_ref[...]

    return window


def forward_kernel(edge, *refs):
    if edge:
        (query_ref, own_ref, prev_ref, next_ref, key_mark_ref, query_mark_ref, _, _,
         out_ref, peak_ref, bias, turned, scores, weights, mixed, window) = refs
    else:
        (query_ref, own_ref, key_mark_ref, query_mark_ref,
         out_ref, peak_ref, bias, turned, scores, weights, mixed) = refs
        prev_ref = next_ref = window = None
    width = query_ref.shape[1]
    view = take_window(edge, pl.program_id(0), prev_ref, own_ref, next_ref, window)
    fill_mask(key_mark_ref, query_mark_ref, bias)
    turned[...] = view[:, width : 2 * width].T
    factor = SCORE_SCALE * LOG2E

    def pair(index, carry):
        for odd in range(2):
            head = 2 * index + odd
            first, inside = head_lanes(head, width)
            query = masked(query_ref, first, inside)
            peak = jnp.full((8, BLOCK), -3e38, F32)
            for start in range(0, SPAN, CHUNK):
                rows = slice(start, start + CHUNK)
                score = dot_rows(view[rows, pl.ds(first, 256)], query) * factor + bias[rows, :]
                scores[odd, rows, :] = score
                peak = jnp.maximum(peak, jnp.max(score.reshape(CHUNK // 8, 8, BLOCK), axis=0))
            peak = jnp.max(peak, axis=0, keepdims=True)
            total = jnp.zeros((8, BLOCK), F32)
            for start in range(0, SPAN, CHUNK):
                rows = slice(start, start + CHUNK)
                power = jnp.exp2(scores[odd, rows, :] - peak)
                total = total + jnp.sum(power.reshape(CHUNK // 8, 8, BLOCK), axis=0)
                weights[odd, rows, :] = power.astype(BF)
            total = jnp.sum(total, axis=0, keepdims=True)
            base = pl.multiple_of(index * 2 * HEAD, 16)
            value = turned[pl.ds(pl.multiple_of(base + 64 * odd, 16), 80), :]
            part = dot_plain(value, weights[odd]) * (1.0 / total)
            mixed[pl.ds(pl.multiple_of(base + HEAD * odd, 8), HEAD), :] = part[8 * odd : 8 * odd + HEAD]
            peak_ref[pl.ds(head, 1), :] = peak + jnp.log2(total)
        return carry

    lax.fori_loop(0, HEADS // 2, pair, 0)
    out_ref[...] = mixed[...].T.astype(BF)


def backward_kernel(edge, *refs):
    if edge:
        (query_ref, out_ref, grad_ref, peak_ref, own_ref, prev_ref, next_ref, key_mark_ref, query_mark_ref,
         grad_query_ref, rim_low_ref, rim_high_ref, grad_own_ref,
         bias, turned, weights, signals, mixed, delta, window, total) = refs
    else:
        (query_ref, out_ref, grad_ref, peak_ref, own_ref, key_mark_ref, query_mark_ref, edge_ref, _,
         grad_query_ref, grad_own_ref,
         bias, turned, weights, signals, mixed, delta, sem) = refs
        prev_ref = next_ref = window = None
    width = query_ref.shape[1]
    step = pl.program_id(0)
    view = take_window(edge, step, prev_ref, own_ref, next_ref, window)
    inner = SPAN - MAXLEN
    if edge:
        total[...] = jnp.zeros_like(total)
        sums = total
    else:
        rows = grad_own_ref.shape[0]

        @pl.when(step == 0)
        def _():
            low = pltpu.make_async_copy(edge_ref.at[0], grad_own_ref.at[pl.ds(0, inner)], sem.at[0])
            high = pltpu.make_async_copy(
                edge_ref.at[1], grad_own_ref.at[pl.ds(rows - inner, inner)], sem.at[1]
            )
            low.start()
            high.start()
            grad_own_ref[inner : rows - inner, :] = jnp.zeros((rows - 2 * inner, 2 * width), F32)
            low.wait()
            high.wait()

        sums = grad_own_ref.at[pl.ds(pl.multiple_of(step * BLOCK + BLOCK - MAXLEN, 64), SPAN)]
    fill_mask(key_mark_ref, query_mark_ref, bias)
    turned[...] = view[:, 0:width].T
    product = out_ref[...].astype(F32) * grad_ref[...].astype(F32)
    high = product.astype(BF)
    low = (product - high.astype(F32)).astype(BF)
    of_head = (
        lax.broadcasted_iota(jnp.int32, (HEADS, width), 1) // HEAD
        == lax.broadcasted_iota(jnp.int32, (HEADS, width), 0)
    ).astype(BF)
    delta[...] = dot_rows(of_head, high) + dot_rows(of_head, low)
    factor = SCORE_SCALE * LOG2E

    def pair(index, carry):
        for odd in range(2):
            head = 2 * index + odd
            first, inside = head_lanes(head, width)
            query = masked(query_ref, first, inside)
            grad = masked(grad_ref, first, inside)
            peak = peak_ref[pl.ds(head, 1), :]
            mean = delta[pl.ds(head, 1), :]
            for start in range(0, SPAN, CHUNK):
                rows = slice(start, start + CHUNK)
                score = dot_rows(view[rows, pl.ds(first, 256)], query) * factor
                power = jnp.exp2(score + (bias[rows, :] - peak))
                slope = dot_rows(view[rows, pl.ds(first + width, 256)], grad)
                low = power.astype(BF)
                signal = (power * (slope - mean)).astype(BF)
                signals[odd, rows, :] = signal
                sums[rows, pl.ds(first, 256)] += dot_plain(signal, query)
                sums[rows, pl.ds(first + width, 256)] += dot_plain(low, grad)
            base = pl.multiple_of(index * 2 * HEAD, 16)
            key = turned[pl.ds(pl.multiple_of(base + 64 * odd, 16), 80), :]
            part = dot_plain(key, signals[odd]) * SCORE_SCALE
            mixed[pl.ds(pl.multiple_of(base + HEAD * odd, 8), HEAD), :] = part[8 * odd : 8 * odd + HEAD]
        return carry

    lax.fori_loop(0, HEADS // 2, pair, 0)
    grad_query_ref[...] = mixed[...].T.astype(BF)
    if edge:

        @pl.when(step == 0)
        def _():
            rim_low_ref[:, :width] = (total[0:MAXLEN, :width] * SCORE_SCALE).astype(BF)
            rim_low_ref[:, width:] = total[0:MAXLEN, width:].astype(BF)
            grad_own_ref[0] = total[MAXLEN:SPAN, :]

        @pl.when(step == 1)
        def _():
            rim_high_ref[:, :width] = (total[inner:SPAN, :width] * SCORE_SCALE).astype(BF)
            rim_high_ref[:, width:] = total[inner:SPAN, width:].astype(BF)
            grad_own_ref[0] = total[0:inner, :]
    else:

        @pl.when(step == pl.num_programs(0) - 1)
        def _():
            grad_own_ref[:, :width] = grad_own_ref[:, :width] * SCORE_SCALE


def mark_windows(marker, marker_prev, marker_next):
    wide = jnp.concatenate([marker_prev, marker, marker_next])
    count = marker.shape[0] // BLOCK
    keys = jnp.stack([wide[i * BLOCK : i * BLOCK + SPAN] for i in range(count)])[:, None, :]
    return keys, marker.reshape(count, 1, BLOCK)


def whole(shape):
    return pl.BlockSpec(shape, lambda i: (0,) * len(shape))


def attention_calls(rows, width):
    count = rows // BLOCK
    last = count - 1
    inner = SPAN - MAXLEN
    scratch = [
        pltpu.VMEM((SPAN, BLOCK), F32),
        pltpu.VMEM((width, SPAN), BF),
    ]
    elements = SPAN * BLOCK * HEADS

    def block_specs(edge):
        at = (lambda i: i * last) if edge else (lambda i: i + 1)
        row_block = pl.BlockSpec((BLOCK, width), lambda i: (at(i), 0))
        lane_block = pl.BlockSpec((HEADS, BLOCK), lambda i: (0, at(i)))
        key_mark = pl.BlockSpec((1, 1, SPAN), lambda i: (at(i), 0, 0))
        query_mark = pl.BlockSpec((1, 1, BLOCK), lambda i: (at(i), 0, 0))
        return row_block, lane_block, key_mark, query_mark

    any_spec = pl.BlockSpec(memory_space=pl.ANY)
    params = pltpu.CompilerParams(vmem_limit_bytes=VMEM, dimension_semantics=("arbitrary",))

    def forward(edge, queries, key_value, marks, halo=(), before=()):
        row_block, lane_block, key_mark, query_mark = block_specs(edge)
        steps = 2 if edge else count - 2
        in_specs = [row_block, whole((rows, 2 * width))]
        in_specs += [whole((MAXLEN, 2 * width))] * len(halo)
        in_specs += [key_mark, query_mark] + [any_spec] * len(before)
        extra = [pltpu.VMEM((SPAN, 2 * width), BF)] if edge else []
        return pl.pallas_call(
            functools.partial(forward_kernel, edge),
            grid=(steps,),
            in_specs=in_specs,
            out_specs=[row_block, lane_block],
            out_shape=[
                jax.ShapeDtypeStruct((rows, width), BF),
                jax.ShapeDtypeStruct((HEADS, rows), F32),
            ],
            scratch_shapes=scratch
            + [
                pltpu.VMEM((2, SPAN, BLOCK), F32),
                pltpu.VMEM((2, SPAN, BLOCK), BF),
                pltpu.VMEM((width, BLOCK), F32),
            ]
            + extra,
            input_output_aliases={6: 0, 7: 1} if edge else {},
            compiler_params=params,
            cost_estimate=pl.CostEstimate(
                flops=steps * elements * 1024, bytes_accessed=rows * width * 6, transcendentals=steps * elements
            ),
            name="attend_edge" if edge else "attend_inner",
        )(queries, key_value, *halo, *marks, *before)

    def backward(edge, queries, mixed, grad, peaks, key_value, marks, halo=(), before=()):
        row_block, lane_block, key_mark, query_mark = block_specs(edge)
        steps = 2 if edge else count - 2
        in_specs = [row_block, row_block, row_block, lane_block, whole((rows, 2 * width))]
        in_specs += [whole((MAXLEN, 2 * width))] * len(halo)
        in_specs += [key_mark, query_mark] + [any_spec] * len(before)
        rim = jax.ShapeDtypeStruct((MAXLEN, 2 * width), BF)
        if edge:
            out_specs = [row_block, whole(rim.shape), whole(rim.shape),
                         pl.BlockSpec((1, inner, 2 * width), lambda i: (i, 0, 0))]
            out_shape = [jax.ShapeDtypeStruct((rows, width), BF), rim, rim,
                         jax.ShapeDtypeStruct((2, inner, 2 * width), F32)]
            extra = [pltpu.VMEM((SPAN, 2 * width), BF), pltpu.VMEM((SPAN, 2 * width), F32)]
        else:
            out_specs = [row_block, whole((rows, 2 * width))]
            out_shape = [jax.ShapeDtypeStruct((rows, width), BF),
                         jax.ShapeDtypeStruct((rows, 2 * width), F32)]
            extra = [pltpu.SemaphoreType.DMA((2,))]
        return pl.pallas_call(
            functools.partial(backward_kernel, edge),
            grid=(steps,),
            in_specs=in_specs,
            out_specs=out_specs,
            out_shape=out_shape,
            scratch_shapes=scratch
            + [
                pltpu.VMEM((2, SPAN, BLOCK), BF),
                pltpu.VMEM((2, SPAN, BLOCK), BF),
                pltpu.VMEM((width, BLOCK), F32),
                pltpu.VMEM((HEADS, BLOCK), F32),
            ]
            + extra,
            input_output_aliases={} if edge else {8: 0},
            compiler_params=params,
            cost_estimate=pl.CostEstimate(
                flops=steps * elements * 2560, bytes_accessed=rows * width * 16, transcendentals=steps * elements
            ),
            name="attend_back_edge" if edge else "attend_back_inner",
        )(queries, mixed, grad, peaks, key_value, *halo, *marks, *before)

    return forward, backward


epsilon = 1e-06
highest = lax.Precision.HIGHEST


def partners(axis, bit):
    return [(i, i ^ bit) for i in range(lax.axis_size(axis))]


def halve(blocks, axis, bit):
    mine = (lax.axis_index(axis) // bit) % 2
    kept = lax.dynamic_index_in_dim(blocks, mine, 0, keepdims=False)
    sent = lax.dynamic_index_in_dim(blocks, 1 - mine, 0, keepdims=False)
    got = lax.ppermute(sent.astype(jnp.bfloat16), axis, partners(axis, bit))
    return kept.astype(jnp.float32) + got.astype(jnp.float32)


def share_of_sum(partial_sum):
    rows, columns = partial_sum.shape
    count, seq_count = lax.axis_size("dp"), lax.axis_size("seq")
    total = partial_sum.reshape(count, rows // count, columns)
    bit = 1
    while bit < count:
        total = total.reshape(-1, 2, *total.shape[1:]).swapaxes(0, 1)
        total = halve(total, "dp", bit)
        bit *= 2
    total = total.reshape(rows // count, seq_count, columns // seq_count).astype(jnp.bfloat16).swapaxes(0, 1)
    bit = 1
    while bit < seq_count:
        total = total.reshape(-1, 2, *total.shape[1:]).swapaxes(0, 1)
        total = halve(total, "seq", bit)
        bit *= 2
    return total[0]


def layer_norm(token_rows):
    centred = token_rows - jnp.mean(token_rows, axis=-1, keepdims=True)
    inverse = lax.rsqrt(jnp.mean(centred * centred, axis=-1, keepdims=True) + epsilon)
    return (centred * inverse, inverse)


def norm_back(upstream, normed, inverse):
    return inverse * (
        upstream
        - jnp.mean(upstream, axis=-1, keepdims=True)
        - normed * jnp.mean(upstream * normed, axis=-1, keepdims=True)
    )


def outer_sum(first_matrix, second_matrix):
    return lax.dot_general(
        first_matrix, second_matrix, (((0,), (0,)), ((), ())), preferred_element_type=jnp.float32
    )


def back_dot(gradient, matrix):
    return lax.dot_general(
        gradient, matrix, (((1,), (1,)), ((), ())), preferred_element_type=jnp.float32
    )


def shards(
    tokens,
    segments,
    condition,
    cotangent,
    modulation_weight,
    modulation_bias,
    input_weight,
    query_value_bias,
    output_weight,
    output_bias,
    expand_weight,
    expand_bias,
    contract_weight,
    contract_bias,
):
    modulation_full, input_full, output_full, expand_full, contract_full = (
        lax.all_gather(modulation_weight, "dp", axis=0, tiled=True),
        lax.all_gather(input_weight, "dp", axis=0, tiled=True),
        lax.all_gather(output_weight, "dp", axis=0, tiled=True),
        lax.all_gather(expand_weight, "dp", axis=0, tiled=True),
        lax.all_gather(contract_weight, "dp", axis=0, tiled=True),
    )
    token_rows = tokens[0].astype(jnp.float32)
    segment = segments[0]
    conditions = condition[0]
    grad_out = cotangent[0].astype(jnp.float32)
    row_count, model_width = token_rows.shape
    images = conditions.shape[0]
    first_image = jnp.minimum(segment[0], images - WIN)
    window = lax.dynamic_slice_in_dim(conditions, first_image, WIN, 0).astype(jnp.float32)
    image_select = (
        (segment - first_image)[:, None] == jnp.arange(WIN, dtype=jnp.int32)[None, :]
    ).astype(jnp.float32)
    silu_low = jax.nn.silu(window).astype(jnp.bfloat16)
    modulation = jnp.dot(
        silu_low, modulation_full, preferred_element_type=jnp.float32
    ) + modulation_bias.astype(jnp.float32)
    per_row = jnp.dot(image_select, modulation, precision=highest)
    shift_mixer, scale_mixer, gate_mixer, shift_feed, scale_feed, gate_feed = jnp.split(
        per_row, 6, axis=1
    )
    normed_attn, inverse_attn = layer_norm(token_rows)
    input_attn = (normed_attn * (1.0 + scale_mixer) + shift_mixer).astype(jnp.bfloat16)
    packed = jnp.dot(input_attn, input_full, preferred_element_type=jnp.float32)
    bias_values = query_value_bias.astype(jnp.float32)
    queries = (packed[:, :model_width] + bias_values[:model_width]).astype(jnp.bfloat16)
    key_rows = packed[:, model_width : 2 * model_width].astype(jnp.bfloat16)
    values = (packed[:, 2 * model_width :] + bias_values[model_width:]).astype(jnp.bfloat16)
    key_value = jnp.concatenate([key_rows, values], axis=1)
    marker = segment + 1
    seq_count = lax.axis_size("seq")
    onward = [(i, i + 1) for i in range(seq_count - 1)]
    back = [(i + 1, i) for i in range(seq_count - 1)]
    marks = mark_windows(
        marker,
        lax.ppermute(marker[row_count - MAXLEN :], "seq", onward),
        lax.ppermute(marker[:MAXLEN], "seq", back),
    )
    halo = (
        lax.ppermute(key_value[row_count - MAXLEN :], "seq", onward),
        lax.ppermute(key_value[:MAXLEN], "seq", back),
    )
    attend, attend_back = attention_calls(row_count, model_width)
    inner_part = attend(False, queries, key_value, marks)
    attn_mixed, row_peaks = attend(True, queries, key_value, marks, halo, inner_part)
    attn_out = jnp.dot(
        attn_mixed, output_full, preferred_element_type=jnp.float32
    ) + output_bias.astype(jnp.float32)
    middle = token_rows + gate_mixer * attn_out
    normed_feed, inverse_feed = layer_norm(middle)
    input_feed = (normed_feed * (1.0 + scale_feed) + shift_feed).astype(jnp.bfloat16)
    hidden = jnp.dot(
        input_feed, expand_full, preferred_element_type=jnp.float32
    ) + expand_bias.astype(jnp.float32)
    active, gelu_back = jax.vjp(partial(jax.nn.gelu, approximate=True), hidden)
    active_low = active.astype(jnp.bfloat16)
    feed_out = jnp.dot(
        active_low, contract_full, preferred_element_type=jnp.float32
    ) + contract_bias.astype(jnp.float32)
    layer_out = (middle + gate_feed * feed_out).astype(jnp.bfloat16)
    grad_feed = (grad_out * gate_feed).astype(jnp.bfloat16)
    grad_gate_feed = grad_out * feed_out
    grad_contract_weight = outer_sum(active_low, grad_feed)
    grad_contract_bias = jnp.sum(grad_feed.astype(jnp.float32), axis=0)
    grad_active = back_dot(grad_feed, contract_full)
    grad_hidden = gelu_back(grad_active)[0].astype(jnp.bfloat16)
    grad_expand_weight = outer_sum(input_feed, grad_hidden)
    grad_expand_bias = jnp.sum(grad_hidden.astype(jnp.float32), axis=0)
    grad_input_feed = back_dot(grad_hidden, expand_full)
    grad_scale_feed = grad_input_feed * normed_feed
    grad_middle = grad_out + norm_back(
        grad_input_feed * (1.0 + scale_feed), normed_feed, inverse_feed
    )
    grad_gate_mixer = grad_middle * attn_out
    grad_attn = (grad_middle * gate_mixer).astype(jnp.bfloat16)
    grad_output_weight = outer_sum(attn_mixed, grad_attn)
    grad_output_bias = jnp.sum(grad_attn.astype(jnp.float32), axis=0)
    grad_mixed = back_dot(grad_attn, output_full).astype(jnp.bfloat16)
    grad_query_edge, rim_low, rim_high, grad_edge = attend_back(
        True, queries, attn_mixed, grad_mixed, row_peaks, key_value, marks, halo
    )
    from_next = lax.ppermute(rim_low, "seq", back)
    from_prev = lax.ppermute(rim_high, "seq", onward)
    grad_query, own_grad = attend_back(
        False, queries, attn_mixed, grad_mixed, row_peaks, key_value, marks, (), (grad_edge, grad_query_edge)
    )
    own_grad = own_grad.at[:MAXLEN].add(from_prev.astype(jnp.float32))
    own_grad = own_grad.at[row_count - MAXLEN :].add(from_next.astype(jnp.float32))
    grad_packed = jnp.concatenate([grad_query, own_grad.astype(jnp.bfloat16)], axis=1)
    grad_input_weight = outer_sum(input_attn, grad_packed)
    packed_sums = jnp.sum(grad_packed.astype(jnp.float32), axis=0)
    grad_query_value_bias = jnp.concatenate(
        [packed_sums[:model_width], packed_sums[2 * model_width :]]
    )
    grad_input_attn = back_dot(grad_packed, input_full)
    grad_scale_mixer = grad_input_attn * normed_attn
    grad_rows = grad_middle + norm_back(
        grad_input_attn * (1.0 + scale_mixer), normed_attn, inverse_attn
    )
    grad_per_row = jnp.concatenate(
        [
            grad_input_attn,
            grad_scale_mixer,
            grad_gate_mixer,
            grad_input_feed,
            grad_scale_feed,
            grad_gate_feed,
        ],
        axis=1,
    )
    window_grads = lax.dot_general(
        image_select, grad_per_row, (((0,), (0,)), ((), ())), precision=highest
    )
    image_grads = lax.dynamic_update_slice_in_dim(
        jnp.zeros((images, window_grads.shape[1]), jnp.float32), window_grads, first_image, 0
    )
    column_grads = lax.psum_scatter(image_grads, "seq", scatter_dimension=1, tiled=True)
    columns = column_grads.shape[1]
    silu_all, silu_all_back = jax.vjp(jax.nn.silu, conditions.astype(jnp.float32))
    cond_act = silu_all.astype(jnp.bfloat16)
    all_grads = lax.all_gather(column_grads, "dp", axis=0, tiled=True)
    all_act = lax.all_gather(cond_act, "dp", axis=0, tiled=True)
    share_rows = modulation_weight.shape[0]
    own_act = lax.dynamic_slice_in_dim(all_act, lax.axis_index("dp") * share_rows, share_rows, 1)
    total_modulation = lax.dot_general(
        own_act.astype(jnp.float32), all_grads, (((0,), (0,)), ((), ())), precision=highest
    )
    own_columns = lax.dynamic_slice_in_dim(
        modulation_full, lax.axis_index("seq") * columns, columns, 1
    )
    grad_condition = silu_all_back(lax.dot_general(
        column_grads, own_columns.astype(jnp.float32), (((1,), (1,)), ((), ())), precision=highest
    ))[0]
    grad_condition = lax.psum_scatter(grad_condition, "seq", scatter_dimension=0, tiled=True)
    grad_modulation_bias = jnp.sum(window_grads, axis=0)
    total_contract = share_of_sum(grad_contract_weight)
    total_expand = share_of_sum(grad_expand_weight)
    total_output = share_of_sum(grad_output_weight)
    total_input = share_of_sum(grad_input_weight)
    bias_modulation, bias_query_value, bias_output, bias_expand, bias_contract = lax.psum(
        (
            grad_modulation_bias,
            grad_query_value_bias,
            grad_output_bias,
            grad_expand_bias,
            grad_contract_bias,
        ),
        ("dp", "seq"),
    )
    return (
        layer_out[None],
        grad_rows[None],
        grad_condition[None],
        total_modulation,
        bias_modulation,
        total_input,
        bias_query_value,
        total_output,
        bias_output,
        total_expand,
        bias_expand,
        total_contract,
        bias_contract,
    )


def solution(mesh):
    in_specs = (
        P("dp", "seq", None),
        P("dp", "seq"),
        P("dp", None, None),
        P("dp", "seq", None),
        P("dp", None),
        P(),
        P("dp", None),
        P(),
        P("dp", None),
        P(),
        P("dp", None),
        P(),
        P("dp", None),
        P(),
    )
    out_specs = (
        P("dp", "seq", None),
        P("dp", "seq", None),
        P("dp", "seq", None),
        P("dp", "seq"),
        P(),
        P("dp", "seq"),
        P(),
        P("dp", "seq"),
        P(),
        P("dp", "seq"),
        P(),
        P("dp", "seq"),
        P(),
    )
    return jax.shard_map(shards, mesh=mesh, in_specs=in_specs, out_specs=out_specs, check_vma=False)
```

```python
import functools
import math

import jax
import jax.numpy as jnp
from jax import lax
from jax.experimental import pallas as pl
from jax.experimental.pallas import tpu as pltpu
from jax.sharding import PartitionSpec as P

WIN = 24
WIN_PAD = 32
BEFORE = 3
TERMS = 128
HEADS = 16
MAXLEN = 192
HEAD = 72
BLOCK = 256
SPAN = BLOCK + 2 * MAXLEN
CHUNK = 128
BF, F32 = jnp.bfloat16, jnp.float32
SCORE_SCALE = 1.0 / math.sqrt(HEAD)
LOG2E = 1.4426950408889634
VMEM = 60 * 1024 * 1024


def dot_rows(left, right):
    return lax.dot_general(left, right, (((1,), (1,)), ((), ())), preferred_element_type=F32)


def dot_plain(left, right):
    return jnp.dot(left, right, preferred_element_type=F32)


def fill_mask(key_mark_ref, query_mark_ref, bias):
    marks = jnp.broadcast_to(key_mark_ref[0].astype(F32), (CHUNK, SPAN))
    columns = marks.T
    query = query_mark_ref[0].astype(F32)
    for lane in range(0, BLOCK, CHUNK):
        bias[:, lane : lane + CHUNK] = jnp.where(
            columns == query[:, lane : lane + CHUNK], 0.0, -1e30
        )


def head_lanes(head, width):
    first = jnp.minimum((head * HEAD) // 128 * 128, width - 256)
    lanes = lax.broadcasted_iota(jnp.int32, (1, 256), 1) + first
    inside = (lanes >= head * HEAD) & (lanes < (head + 1) * HEAD)
    return pl.multiple_of(first, 128), inside


def masked(ref, first, inside):
    block = ref[:, pl.ds(first, 256)]
    return jnp.where(inside, block, jnp.zeros_like(block))


def fill_window(block, last, pair_ref, window):
    rows = pair_ref.shape[0] - 2 * MAXLEN
    inner = SPAN - MAXLEN

    @pl.when(block == 0)
    def _():
        window[0:MAXLEN, :] = pair_ref[rows : rows + MAXLEN, :]
        window[MAXLEN:SPAN, :] = pair_ref[0:inner, :]

    @pl.when((block > 0) & (block < last))
    def _():
        window[...] = pair_ref[pl.ds(pl.multiple_of(block * BLOCK - MAXLEN, 64), SPAN), :]

    @pl.when(block == last)
    def _():
        window[0:inner, :] = pair_ref[rows - inner : rows, :]
        window[inner:SPAN, :] = pair_ref[rows + MAXLEN : rows + 2 * MAXLEN, :]


def forward_kernel(query_ref, pair_ref, key_mark_ref, query_mark_ref,
                   out_ref, peak_ref, bias, turned, scores, weights, mixed, view):
    width = query_ref.shape[1]
    fill_window(pl.program_id(0), pl.num_programs(0) - 1, pair_ref, view)
    fill_mask(key_mark_ref, query_mark_ref, bias)
    turned[...] = view[:, width : 2 * width].T
    factor = SCORE_SCALE * LOG2E

    def pair(index, carry):
        for odd in range(2):
            head = 2 * index + odd
            first, inside = head_lanes(head, width)
            query = masked(query_ref, first, inside)
            peak = jnp.full((8, BLOCK), -3e38, F32)
            for start in range(0, SPAN, CHUNK):
                rows = slice(start, start + CHUNK)
                score = dot_rows(view[rows, pl.ds(first, 256)], query) * factor + bias[rows, :]
                scores[odd, rows, :] = score
                peak = jnp.maximum(peak, jnp.max(score.reshape(CHUNK // 8, 8, BLOCK), axis=0))
            peak = jnp.max(peak, axis=0, keepdims=True)
            total = jnp.zeros((8, BLOCK), F32)
            for start in range(0, SPAN, CHUNK):
                rows = slice(start, start + CHUNK)
                power = jnp.exp2(scores[odd, rows, :] - peak)
                total = total + jnp.sum(power.reshape(CHUNK // 8, 8, BLOCK), axis=0)
                weights[odd, rows, :] = power.astype(BF)
            total = jnp.sum(total, axis=0, keepdims=True)
            base = pl.multiple_of(index * 2 * HEAD, 16)
            value = turned[pl.ds(pl.multiple_of(base + 64 * odd, 16), 80), :]
            part = dot_plain(value, weights[odd]) * (1.0 / total)
            mixed[pl.ds(pl.multiple_of(base + HEAD * odd, 8), HEAD), :] = part[8 * odd : 8 * odd + HEAD]
            peak_ref[pl.ds(head, 1), :] = peak + jnp.log2(total)
        return carry

    lax.fori_loop(0, HEADS // 2, pair, 0)
    out_ref[...] = mixed[...].T.astype(BF)


def backward_kernel(edge, *refs):
    if edge:
        (query_ref, out_ref, grad_ref, peak_ref, pair_ref, key_mark_ref, query_mark_ref,
         grad_query_ref, rim_low_ref, rim_high_ref, grad_own_ref,
         bias, turned, weights, signals, mixed, delta, view, total) = refs
    else:
        (query_ref, out_ref, grad_ref, peak_ref, pair_ref, key_mark_ref, query_mark_ref, edge_ref, _,
         grad_query_ref, grad_own_ref,
         bias, turned, weights, signals, mixed, delta, view, sem) = refs
    width = query_ref.shape[1]
    step = pl.program_id(0)
    last = (pair_ref.shape[0] - 2 * MAXLEN) // BLOCK - 1
    fill_window(step * last if edge else step + 1, last, pair_ref, view)
    inner = SPAN - MAXLEN
    if edge:
        total[...] = jnp.zeros_like(total)
        sums = total
    else:
        rows = grad_own_ref.shape[0]

        @pl.when(step == 0)
        def _():
            low = pltpu.make_async_copy(edge_ref.at[0], grad_own_ref.at[pl.ds(0, inner)], sem.at[0])
            high = pltpu.make_async_copy(
                edge_ref.at[1], grad_own_ref.at[pl.ds(rows - inner, inner)], sem.at[1]
            )
            low.start()
            high.start()
            grad_own_ref[inner : rows - inner, :] = jnp.zeros((rows - 2 * inner, 2 * width), F32)
            low.wait()
            high.wait()

        sums = grad_own_ref.at[pl.ds(pl.multiple_of(step * BLOCK + BLOCK - MAXLEN, 64), SPAN)]
    fill_mask(key_mark_ref, query_mark_ref, bias)
    turned[...] = view[:, 0:width].T
    product = out_ref[...].astype(F32) * grad_ref[...].astype(F32)
    high = product.astype(BF)
    low = (product - high.astype(F32)).astype(BF)
    of_head = (
        lax.broadcasted_iota(jnp.int32, (HEADS, width), 1) // HEAD
        == lax.broadcasted_iota(jnp.int32, (HEADS, width), 0)
    ).astype(BF)
    delta[...] = dot_rows(of_head, high) + dot_rows(of_head, low)
    factor = SCORE_SCALE * LOG2E

    def pair(index, carry):
        for odd in range(2):
            head = 2 * index + odd
            first, inside = head_lanes(head, width)
            query = masked(query_ref, first, inside)
            grad = masked(grad_ref, first, inside)
            peak = peak_ref[pl.ds(head, 1), :]
            mean = delta[pl.ds(head, 1), :]
            for start in range(0, SPAN, CHUNK):
                rows = slice(start, start + CHUNK)
                score = dot_rows(view[rows, pl.ds(first, 256)], query) * factor
                power = jnp.exp2(score + (bias[rows, :] - peak))
                slope = dot_rows(view[rows, pl.ds(first + width, 256)], grad)
                low = power.astype(BF)
                signal = (power * (slope - mean)).astype(BF)
                signals[odd, rows, :] = signal
                sums[rows, pl.ds(first, 256)] += dot_plain(signal, query)
                sums[rows, pl.ds(first + width, 256)] += dot_plain(low, grad)
            base = pl.multiple_of(index * 2 * HEAD, 16)
            key = turned[pl.ds(pl.multiple_of(base + 64 * odd, 16), 80), :]
            part = dot_plain(key, signals[odd]) * SCORE_SCALE
            mixed[pl.ds(pl.multiple_of(base + HEAD * odd, 8), HEAD), :] = part[8 * odd : 8 * odd + HEAD]
        return carry

    lax.fori_loop(0, HEADS // 2, pair, 0)
    grad_query_ref[...] = mixed[...].T.astype(BF)
    if edge:

        @pl.when(step == 0)
        def _():
            rim_low_ref[:, :width] = (total[0:MAXLEN, :width] * SCORE_SCALE).astype(BF)
            rim_low_ref[:, width:] = total[0:MAXLEN, width:].astype(BF)
            grad_own_ref[0] = total[MAXLEN:SPAN, :]

        @pl.when(step == 1)
        def _():
            rim_high_ref[:, :width] = (total[inner:SPAN, :width] * SCORE_SCALE).astype(BF)
            rim_high_ref[:, width:] = total[inner:SPAN, width:].astype(BF)
            grad_own_ref[0] = total[0:inner, :]
    else:

        @pl.when(step == pl.num_programs(0) - 1)
        def _():
            grad_own_ref[:, :width] = grad_own_ref[:, :width] * SCORE_SCALE


def mark_windows(marker, marker_prev, marker_next):
    wide = jnp.concatenate([marker_prev, marker, marker_next])
    count = marker.shape[0] // BLOCK
    keys = jnp.stack([wide[i * BLOCK : i * BLOCK + SPAN] for i in range(count)])[:, None, :]
    return keys, marker.reshape(count, 1, BLOCK)


def whole(shape):
    return pl.BlockSpec(shape, lambda i: (0,) * len(shape))


def attention_calls(rows, width):
    count = rows // BLOCK
    last = count - 1
    inner = SPAN - MAXLEN
    scratch = [
        pltpu.VMEM((SPAN, BLOCK), F32),
        pltpu.VMEM((width, SPAN), BF),
    ]
    elements = SPAN * BLOCK * HEADS

    def block_specs(at):
        row_block = pl.BlockSpec((BLOCK, width), lambda i: (at(i), 0))
        lane_block = pl.BlockSpec((HEADS, BLOCK), lambda i: (0, at(i)))
        key_mark = pl.BlockSpec((1, 1, SPAN), lambda i: (at(i), 0, 0))
        query_mark = pl.BlockSpec((1, 1, BLOCK), lambda i: (at(i), 0, 0))
        return row_block, lane_block, key_mark, query_mark

    any_spec = pl.BlockSpec(memory_space=pl.ANY)
    params = pltpu.CompilerParams(vmem_limit_bytes=VMEM, dimension_semantics=("arbitrary",))
    pairs = once((rows + 2 * MAXLEN, 2 * width))
    view = pltpu.VMEM((SPAN, 2 * width), BF)

    def forward(queries, key_value, marks, after):
        row_block, lane_block, key_mark, query_mark = block_specs(lambda i: i)
        return pl.pallas_call(
            skipping(forward_kernel, 4, len(after)),
            grid=(count,),
            in_specs=[row_block, pairs, key_mark, query_mark] + [any_spec] * len(after),
            out_specs=[row_block, lane_block],
            out_shape=[
                jax.ShapeDtypeStruct((rows, width), BF),
                jax.ShapeDtypeStruct((HEADS, rows), F32),
            ],
            scratch_shapes=scratch
            + [
                pltpu.VMEM((2, SPAN, BLOCK), F32),
                pltpu.VMEM((2, SPAN, BLOCK), BF),
                pltpu.VMEM((width, BLOCK), F32),
                view,
            ],
            compiler_params=params,
            cost_estimate=cost(11.5 * count),
            name="attend",
        )(queries, key_value, *marks, *after)

    def backward(edge, queries, mixed, grad, peaks, key_value, marks, before=(), after=()):
        row_block, lane_block, key_mark, query_mark = block_specs(
            (lambda i: i * last) if edge else (lambda i: i + 1)
        )
        steps = 2 if edge else count - 2
        in_specs = [row_block, row_block, row_block, lane_block, pairs]
        in_specs += [key_mark, query_mark] + [any_spec] * (len(before) + len(after))
        rim = jax.ShapeDtypeStruct((MAXLEN, 2 * width), BF)
        if edge:
            out_specs = [row_block, whole(rim.shape), whole(rim.shape),
                         pl.BlockSpec((1, inner, 2 * width), lambda i: (i, 0, 0))]
            out_shape = [jax.ShapeDtypeStruct((rows, width), BF), rim, rim,
                         jax.ShapeDtypeStruct((2, inner, 2 * width), F32)]
            extra = [view, pltpu.VMEM((SPAN, 2 * width), F32)]
        else:
            out_specs = [row_block, whole((rows, 2 * width))]
            out_shape = [jax.ShapeDtypeStruct((rows, width), BF),
                         jax.ShapeDtypeStruct((rows, 2 * width), F32)]
            extra = [view, pltpu.SemaphoreType.DMA((2,))]
        return pl.pallas_call(
            skipping(functools.partial(backward_kernel, edge), 7 + len(before), len(after)),
            grid=(steps,),
            in_specs=in_specs,
            out_specs=out_specs,
            out_shape=out_shape,
            scratch_shapes=scratch
            + [
                pltpu.VMEM((2, SPAN, BLOCK), BF),
                pltpu.VMEM((2, SPAN, BLOCK), BF),
                pltpu.VMEM((width, BLOCK), F32),
                pltpu.VMEM((HEADS, BLOCK), F32),
            ]
            + extra,
            input_output_aliases={} if edge else {8: 0},
            compiler_params=params,
            cost_estimate=cost(2.2 * steps),
            name="attend_back_edge" if edge else "attend_back_inner",
        )(queries, mixed, grad, peaks, key_value, *marks, *before, *after)

    return forward, backward


BANDS = 4
EPSILON = 1e-06
ROOT = math.sqrt(2.0 / math.pi)
CUBE = 0.044715


def skipping(kernel, first, count):
    return lambda *refs: kernel(*refs[:first], *refs[first + count :])


def once(shape):
    return pl.BlockSpec(shape, lambda i, *_: (0,) * len(shape), pipeline_mode=pl.Buffered(buffer_count=1))


def rows_of(rows, width):
    return pl.BlockSpec((rows, width), lambda i, *_: (i, 0))


def kernel_params():
    return pltpu.CompilerParams(vmem_limit_bytes=VMEM, dimension_semantics=("arbitrary",))


def cost(microseconds):
    return pl.CostEstimate(flops=int(microseconds * 1.1e9), bytes_accessed=int(microseconds * 3e6), transcendentals=0)


def dot_turned(left, right):
    return lax.dot_general(left, right, (((0,), (0,)), ((), ())), preferred_element_type=F32)


def spread(select, parts_ref, part, width):
    return dot_plain(select, parts_ref[:, part * width : (part + 1) * width])


def normalise(block):
    centred = block - jnp.mean(block, axis=-1, keepdims=True)
    inverse = lax.rsqrt(jnp.mean(centred * centred, axis=-1, keepdims=True) + EPSILON)
    return centred * inverse, inverse


def norm_back(upstream, normed, inverse):
    return inverse * (
        upstream
        - jnp.mean(upstream, axis=-1, keepdims=True)
        - normed * jnp.mean(upstream * normed, axis=-1, keepdims=True)
    )


def image_sum(gather, block):
    high = block.astype(BF)
    low = (block - high.astype(F32)).astype(BF)
    return dot_plain(gather, high) + dot_plain(gather, low)


def column_sum(block):
    rows, width = block.shape
    return jnp.sum(block.reshape(rows // 8, 8, width), axis=0)


def piece_copies(place_ref, piece_refs, full, sems):
    copies = []
    for index, piece in enumerate(piece_refs):
        rows = piece.shape[0]
        start = pl.multiple_of(place_ref[index] * 16, 16)
        copies.append(pltpu.make_async_copy(piece, full.at[pl.ds(start, rows)], sems.at[index]))
    return copies


def begin_pieces(place_ref, piece_refs, full, sems):
    @pl.when(pl.program_id(0) == 0)
    def _():
        for copy in piece_copies(place_ref, piece_refs, full, sems):
            copy.start()


def end_pieces(place_ref, piece_refs, full, sems):
    @pl.when(pl.program_id(0) == 0)
    def _():
        for copy in piece_copies(place_ref, piece_refs, full, sems):
            copy.wait()


def project_kernel(own_rows, tokens_ref, select_ref, parts_ref, bias_ref, weight_ref, input_ref, query_ref, pair_ref):
    width = tokens_ref.shape[1]
    select = select_ref[...]
    normed, _ = normalise(tokens_ref[...].astype(F32))
    shift = spread(select, parts_ref, 0, width)
    scale = spread(select, parts_ref, 1, width)
    rows = (normed * (1.0 + scale) + shift).astype(BF)
    input_ref[...] = rows

    @pl.when(pl.program_id(0) * tokens_ref.shape[0] < own_rows)
    def _():
        query_ref[...] = (dot_plain(rows, weight_ref[:, :width]) + bias_ref[:, :width]).astype(BF)

    pair_ref[:, :width] = dot_plain(rows, weight_ref[:, width : 2 * width]).astype(BF)
    pair_ref[:, width:] = (dot_plain(rows, weight_ref[:, 2 * width :]) + bias_ref[:, width:]).astype(BF)


def project(weight, own_rows, tokens, select, parts, bias):
    rows, width = tokens.shape
    band = rows // BANDS
    return pl.pallas_call(
        functools.partial(project_kernel, own_rows),
        grid=(BANDS,),
        in_specs=[
            rows_of(band, width),
            rows_of(band, select.shape[1]),
            once(parts.shape),
            once(bias.shape),
            once(weight.shape),
        ],
        out_specs=[rows_of(band, width), rows_of(band, width), rows_of(band, 2 * width)],
        out_shape=[
            jax.ShapeDtypeStruct((rows, width), BF),
            jax.ShapeDtypeStruct((rows, width), BF),
            jax.ShapeDtypeStruct((rows, 2 * width), BF),
        ],
        compiler_params=kernel_params(),
        cost_estimate=cost(25),
        name="project",
    )(tokens, select, parts, bias, weight)


def enter_feed_kernel(count, place_ref, mixed_ref, tokens_ref, cotangent_ref, select_ref, parts_ref, bias_ref, *refs):
    pieces = refs[:count]
    attn_ref, middle_ref, input_ref, grad_feed_ref, full, sems = refs[count:]
    width = tokens_ref.shape[1]
    begin_pieces(place_ref, pieces, full, sems)
    select = select_ref[...]
    gate_mixer = spread(select, parts_ref, 0, width)
    shift = spread(select, parts_ref, 1, width)
    scale = spread(select, parts_ref, 2, width)
    gate_feed = spread(select, parts_ref, 3, width)
    grad_feed_ref[...] = (cotangent_ref[...].astype(F32) * gate_feed).astype(BF)
    end_pieces(place_ref, pieces, full, sems)
    attn = dot_plain(mixed_ref[...], full[...]) + bias_ref[...]
    attn_ref[...] = attn
    middle = tokens_ref[...].astype(F32) + gate_mixer * attn
    middle_ref[...] = middle
    normed, _ = normalise(middle)
    input_ref[...] = (normed * (1.0 + scale) + shift).astype(BF)


def enter_feed(place, pieces, mixed, tokens, cotangent, select, parts, bias, after):
    rows, width = tokens.shape
    band = rows // BANDS
    any_spec = pl.BlockSpec(memory_space=pl.ANY)
    block = rows_of(band, width)
    return pl.pallas_call(
        skipping(functools.partial(enter_feed_kernel, len(pieces)), 7 + len(pieces), len(after)),
        grid_spec=pltpu.PrefetchScalarGridSpec(
            num_scalar_prefetch=1,
            grid=(BANDS,),
            in_specs=[block, block, block, rows_of(band, select.shape[1]), once(parts.shape), once(bias.shape)]
            + [any_spec] * (len(pieces) + len(after)),
            out_specs=[block] * 4,
            scratch_shapes=[pltpu.VMEM((width, width), BF), pltpu.SemaphoreType.DMA((len(pieces),))],
        ),
        out_shape=[jax.ShapeDtypeStruct((rows, width), kind) for kind in (F32, F32, BF, BF)],
        compiler_params=kernel_params(),
        cost_estimate=cost(14),
        name="enter_feed",
    )(place, mixed, tokens, cotangent, select, parts, bias, *pieces, *after)


def feed_kernel(input_ref, grad_ref, expand_ref, contract_ref, bias_ref,
                out_ref, grad_input_ref, expand_grad_ref, contract_grad_ref, bias_grad_ref, grad_sum_ref,
                input_turned, grad_turned, active, hidden_grad):
    step = pl.program_id(0)
    rows, width = input_ref.shape

    @pl.when(step == 0)
    def _():
        input_turned[...] = input_ref[...].T
        grad_turned[...] = grad_ref[...].T
        grad_sum_ref[...] = column_sum(grad_ref[...].astype(F32))
        out_ref[...] = jnp.zeros_like(out_ref)
        grad_input_ref[...] = jnp.zeros_like(grad_input_ref)

    bias_grad_ref[...] = jnp.zeros_like(bias_grad_ref)

    def band(index, carry):
        here = pl.ds(pl.multiple_of(index * BLOCK, BLOCK), BLOCK)
        hidden = dot_plain(input_ref[here, :], expand_ref[...]) + bias_ref[...]
        square = hidden * hidden
        bent = jnp.tanh(ROOT * hidden * (1.0 + CUBE * square))
        half = 0.5 + 0.5 * bent
        active[here, :] = (hidden * half).astype(BF)
        slope = half + (0.5 * ROOT) * hidden * (1.0 - bent * bent) * (1.0 + (3.0 * CUBE) * square)
        pulled = dot_rows(grad_ref[here, :], contract_ref[...])
        low = (pulled * slope).astype(BF)
        hidden_grad[here, :] = low
        bias_grad_ref[...] += column_sum(low.astype(F32))
        out_ref[here, :] += dot_plain(active[here, :], contract_ref[...])
        grad_input_ref[here, :] += dot_rows(low, expand_ref[...])
        return carry

    lax.fori_loop(0, rows // BLOCK, band, 0)
    share = width // 4
    block = expand_grad_ref.shape[4]
    for index in range(4):
        part = dot_plain(input_turned[index * share : (index + 1) * share, :], hidden_grad[...]).astype(BF)
        for owner in range(width // block):
            expand_grad_ref[index, owner % 2, owner // 2] = part[:, owner * block : (owner + 1) * block]
    for index in range(4):
        here = slice(index * share, (index + 1) * share)
        part = dot_plain(grad_turned[here, :], active[...]).astype(BF)
        if len(contract_grad_ref.shape) == 3:
            contract_grad_ref[0, here, :] = part
        else:
            rows = contract_grad_ref.shape[3]
            for start in range(0, share, rows):
                rest, side = divmod((index * share + start) // rows, 2)
                contract_grad_ref[0, side, rest] = part[start : start + rows]


def feed(seq_count, inputs, grad_feed, expand, contract, bias):
    rows, width = inputs.shape
    hidden = expand.shape[1]
    steps = hidden // width
    whole_rows = once((rows, width))
    rest = seq_count // 2
    expand_shape = (4, 2, rest, width // 4, hidden // seq_count)
    if width // seq_count % 16 == 0:
        contract_shape = (steps, 2, rest, width // seq_count, width)
    else:
        contract_shape = (steps, width, width)
    result = pl.pallas_call(
        feed_kernel,
        grid=(steps,),
        in_specs=[
            whole_rows,
            whole_rows,
            pl.BlockSpec((width, width), lambda i: (0, i)),
            pl.BlockSpec((width, width), lambda i: (i, 0)),
            pl.BlockSpec((1, width), lambda i: (0, i)),
        ],
        out_specs=[
            whole_rows,
            whole_rows,
            pl.BlockSpec((4, 2, rest // steps) + expand_shape[3:], lambda i: (0, 0, i, 0, 0)),
            pl.BlockSpec((1,) + contract_shape[1:], lambda i: (i,) + (0,) * (len(contract_shape) - 1)),
            pl.BlockSpec((8, width), lambda i: (0, i)),
            once((8, width)),
        ],
        scratch_shapes=[
            pltpu.VMEM((width, rows), BF),
            pltpu.VMEM((width, rows), BF),
            pltpu.VMEM((rows, width), BF),
            pltpu.VMEM((rows, width), BF),
        ],
        out_shape=[
            jax.ShapeDtypeStruct((rows, width), F32),
            jax.ShapeDtypeStruct((rows, width), F32),
            jax.ShapeDtypeStruct(expand_shape, BF),
            jax.ShapeDtypeStruct(contract_shape, BF),
            jax.ShapeDtypeStruct((8, hidden), F32),
            jax.ShapeDtypeStruct((8, width), F32),
        ],
        compiler_params=kernel_params(),
        cost_estimate=cost(94),
        name="feed",
    )(inputs, grad_feed, expand, contract, bias)
    feed_out, grad_input, expand_grad, contract_grad, expand_sums, feed_sums = result
    if len(contract_shape) == 3:
        contract_grad = contract_grad.reshape(steps, rest, 2, width // seq_count, width).swapaxes(1, 2)
    return feed_out, grad_input, expand_grad, contract_grad, expand_sums, feed_sums


def leave_feed_kernel(count, place_ref, feed_ref, grad_input_ref, middle_ref, attn_ref, cotangent_ref, select_ref,
                      gather_ref, parts_ref, bias_ref, *refs):
    pieces = refs[:count]
    out_ref, grad_middle_ref, grad_attn_ref, grad_mixed_ref, image_ref, sum_ref, full, sems = refs[count:]
    width = middle_ref.shape[1]
    step = pl.program_id(0)
    begin_pieces(place_ref, pieces, full, sems)
    select = select_ref[...]
    gather = gather_ref[...]

    @pl.when(step == 0)
    def _():
        image_ref[...] = jnp.zeros_like(image_ref)
        sum_ref[...] = jnp.zeros_like(sum_ref)

    middle = middle_ref[...]
    grad_out = cotangent_ref[...].astype(F32)
    feed_out = feed_ref[...] + bias_ref[...]
    out_ref[...] = (middle + spread(select, parts_ref, 3, width) * feed_out).astype(BF)
    image_ref[:, 3 * width :] += image_sum(gather, grad_out * feed_out)
    grad_input = grad_input_ref[...]
    image_ref[:, width : 2 * width] += image_sum(gather, grad_input)
    normed, inverse = normalise(middle)
    image_ref[:, 2 * width : 3 * width] += image_sum(gather, grad_input * normed)
    scale = spread(select, parts_ref, 2, width)
    grad_middle = grad_out + norm_back(grad_input * (1.0 + scale), normed, inverse)
    grad_middle_ref[...] = grad_middle
    image_ref[:, :width] += image_sum(gather, grad_middle * attn_ref[...])
    grad_attn = (grad_middle * spread(select, parts_ref, 0, width)).astype(BF)
    grad_attn_ref[...] = grad_attn
    sum_ref[...] += column_sum(grad_attn.astype(F32))
    end_pieces(place_ref, pieces, full, sems)
    grad_mixed_ref[...] = dot_rows(grad_attn, full[...]).astype(BF)


def leave_feed(place, pieces, feed_out, grad_input, middle, attn, cotangent, select, gather, parts, bias, after):
    rows, width = middle.shape
    band = rows // BANDS
    any_spec = pl.BlockSpec(memory_space=pl.ANY)
    block = rows_of(band, width)
    images = gather.shape[0]
    return pl.pallas_call(
        skipping(functools.partial(leave_feed_kernel, len(pieces)), 10 + len(pieces), len(after)),
        grid_spec=pltpu.PrefetchScalarGridSpec(
            num_scalar_prefetch=1,
            grid=(BANDS,),
            in_specs=[block] * 5
            + [rows_of(band, select.shape[1]), pl.BlockSpec((images, band), lambda i, *_: (0, i)),
               once(parts.shape), once(bias.shape)]
            + [any_spec] * (len(pieces) + len(after)),
            out_specs=[block] * 4 + [once((images, 4 * width)), once((8, width))],
            scratch_shapes=[pltpu.VMEM((width, width), BF), pltpu.SemaphoreType.DMA((len(pieces),))],
        ),
        out_shape=[jax.ShapeDtypeStruct((rows, width), kind) for kind in (BF, F32, BF, BF)]
        + [jax.ShapeDtypeStruct((images, 4 * width), F32), jax.ShapeDtypeStruct((8, width), F32)],
        compiler_params=kernel_params(),
        cost_estimate=cost(2.2),
        name="leave_feed",
    )(place, feed_out, grad_input, middle, attn, cotangent, select, gather, parts, bias, *pieces, *after)


def store_owners(out_ref, lead, part, first, block, base):
    columns = part.shape[1]
    at = 0
    while at < columns:
        owner, offset = divmod(first + at, block)
        count = min(block - offset, columns - at)
        rest, side = divmod(owner, 2)
        out_ref[lead, side, rest, :, base + offset : base + offset + count] = part[:, at : at + count]
        at += count


def weight_grad_kernel(input_ref, query_ref, pair_ref, mixed_ref, attn_ref, out_ref, turned):
    step = pl.program_id(0)
    width = query_ref.shape[1]
    share = width // 4
    block = out_ref.shape[4] // 4

    def store(grad_ref, first, block, base):
        for index in range(4):
            part = dot_plain(turned[index * share : (index + 1) * share, :], grad_ref[...]).astype(BF)
            store_owners(out_ref, index, part, first, block, base)

    @pl.when(step == 0)
    def _():
        turned[...] = input_ref[...].T
        store(query_ref, 0, 3 * block, 0)

    for number in (1, 2):

        @pl.when(step == number)
        def _(number=number):
            store(pair_ref, number * width, 3 * block, 0)

    @pl.when(step == 3)
    def _():
        turned[...] = mixed_ref[...].T
        store(attn_ref, 0, block, 3 * block)


def weight_grad(seq_count, inputs, query, pair, mixed, attn, after):
    rows, width = query.shape
    shape = (4, 2, seq_count // 2, width // 4, 4 * width // seq_count)
    whole_rows = once((rows, width))
    return pl.pallas_call(
        skipping(weight_grad_kernel, 5, len(after)),
        grid=(4,),
        in_specs=[
            whole_rows,
            whole_rows,
            pl.BlockSpec((rows, width), lambda i: (0, jnp.clip(i - 1, 0, 1))),
            whole_rows,
            whole_rows,
        ]
        + [pl.BlockSpec(memory_space=pl.ANY)] * len(after),
        out_specs=once(shape),
        scratch_shapes=[pltpu.VMEM((width, rows), BF)],
        out_shape=jax.ShapeDtypeStruct(shape, BF),
        compiler_params=kernel_params(),
        cost_estimate=cost(2),
        name="weight_grad",
    )(inputs, query, pair, mixed, attn, *after)


def leave_kernel(query_ref, pair_ref, tokens_ref, grad_middle_ref, select_ref, gather_ref, parts_ref, weight_ref,
                 feed_images_ref, grad_ref, image_ref, sum_ref):
    width = tokens_ref.shape[1]
    select = select_ref[...]
    gather = gather_ref[...]

    @pl.when(pl.program_id(0) == 0)
    def _():
        image_ref[:, : 2 * width] = jnp.zeros_like(image_ref[:, : 2 * width])
        image_ref[:, 2 * width :] = feed_images_ref[...]
        sum_ref[...] = jnp.zeros_like(sum_ref)

    query = query_ref[...]
    pair = pair_ref[...]
    sum_ref[:, :width] += column_sum(query.astype(F32))
    sum_ref[:, width:] += column_sum(pair[:, width:].astype(F32))
    normed, inverse = normalise(tokens_ref[...].astype(F32))
    scale = spread(select, parts_ref, 1, width)
    grad_input = dot_rows(query, weight_ref[:, :width]) + dot_rows(pair, weight_ref[:, width:])
    image_ref[:, :width] += image_sum(gather, grad_input)
    image_ref[:, width : 2 * width] += image_sum(gather, grad_input * normed)
    grad_ref[...] = grad_middle_ref[...] + norm_back(grad_input * (1.0 + scale), normed, inverse)


def leave(weight, query, pair, tokens, grad_middle, select, gather, parts, feed_images, after):
    rows, width = tokens.shape
    band = rows // BANDS
    block = rows_of(band, width)
    images = gather.shape[0]
    return pl.pallas_call(
        skipping(leave_kernel, 9, len(after)),
        grid=(BANDS,),
        in_specs=[block, rows_of(band, 2 * width), block, block, rows_of(band, select.shape[1]),
                  pl.BlockSpec((images, band), lambda i: (0, i)), once(parts.shape), once(weight.shape),
                  once(feed_images.shape)]
        + [pl.BlockSpec(memory_space=pl.ANY)] * len(after),
        out_specs=[block, once((images, 6 * width)), once((8, 2 * width))],
        out_shape=[
            jax.ShapeDtypeStruct((rows, width), F32),
            jax.ShapeDtypeStruct((images, 6 * width), F32),
            jax.ShapeDtypeStruct((8, 2 * width), F32),
        ],
        compiler_params=kernel_params(),
        cost_estimate=cost(2.5),
        name="leave",
    )(query, pair, tokens, grad_middle, select, gather, parts, weight, feed_images, *after)


def partners(axis, bit):
    return [(i, i ^ bit) for i in range(lax.axis_size(axis))]


def bits_of(axis):
    bit = 1
    while bit < lax.axis_size(axis):
        yield bit
        bit *= 2


def doubled(value, axis, bits=None):
    place = lax.axis_index(axis)
    for bit in bits_of(axis) if bits is None else bits:
        other = lax.ppermute(value, axis, partners(axis, bit))
        mine = (place // bit) % 2
        value = jnp.concatenate([jnp.where(mine == 0, value, other), jnp.where(mine == 0, other, value)])
    return value


def neighbour_groups():
    dp_count, seq_count = lax.axis_size("dp"), lax.axis_size("seq")
    return [
        [d * seq_count + 2 * pair + side for d in range(dp_count) for side in range(2)]
        for pair in range(seq_count // 2)
    ]


def gathered(weight):
    rows = weight.shape[0] // 2
    half = lax.dynamic_slice_in_dim(weight, lax.axis_index("seq") % 2 * rows, rows, 0)
    return lax.all_gather(half, ("dp", "seq"), axis=0, tiled=True, axis_index_groups=neighbour_groups())


def scattered(grad):
    return lax.psum_scatter(
        grad.reshape(-1, *grad.shape[2:]), ("dp", "seq"), scatter_dimension=0, axis_index_groups=neighbour_groups()
    )


def along_rest(rest):
    stages = []
    for bit in list(bits_of("seq"))[1:]:
        pairs = rest.reshape(-1, 2, *rest.shape[1:])
        mine = (lax.axis_index("seq") // bit) % 2
        sent = lax.dynamic_index_in_dim(pairs, 1 - mine, 1, keepdims=False)
        rest = wide(lax.dynamic_index_in_dim(pairs, mine, 1, keepdims=False)) + wide(swapped(sent, "seq", bit))
        stages.append(rest)
    return stages


def gate(value, other):
    first = other[(0,) * other.ndim]
    return jnp.where(first == first, value, jnp.zeros_like(value))


def swapped(value, axis, bit, kind=BF):
    return lax.ppermute(value.astype(kind), axis, partners(axis, bit))


def wide(value):
    return value.astype(F32)


def split_owners(value):
    return value.reshape(2, -1, 2, *value.shape[2:])


def three_terms(value):
    high = lax.reduce_precision(value, 8, 7)
    middle = lax.reduce_precision(value - high, 8, 7)
    low = value - high - middle
    high, middle, low = high.astype(BF), middle.astype(BF), low.astype(BF)
    pad = jnp.zeros((TERMS - 3 * WIN, value.shape[1]), BF)
    return jnp.concatenate([high, middle, low, pad])


def shards(
    tokens,
    segments,
    condition,
    cotangent,
    modulation_weight,
    modulation_bias,
    input_weight,
    query_value_bias,
    output_weight,
    output_bias,
    expand_weight,
    expand_bias,
    contract_weight,
    contract_bias,
):
    token_rows = tokens[0]
    segment = segments[0]
    conditions = condition[0].astype(F32)
    grad_out = cotangent[0]
    row_count, width = token_rows.shape
    images = conditions.shape[0]
    own = lax.axis_index("dp")
    place_in_seq = lax.axis_index("seq")
    seq_count = lax.axis_size("seq")
    onward = [(i, i + 1) for i in range(seq_count - 1)]
    back = [(i + 1, i) for i in range(seq_count - 1)]
    columns = modulation_weight.shape[1] // seq_count
    row = lambda bias: bias.astype(F32)[None, :]

    input_full = gathered(input_weight)
    expand_full = gathered(expand_weight)
    contract_full = gathered(contract_weight)
    silu_all, silu_back = jax.vjp(jax.nn.silu, conditions)
    cond_act = silu_all.astype(BF)
    late = 2 * width
    mixer_columns = late // seq_count
    feed_columns = 4 * width // seq_count
    share_rows = width // 4
    seq_bits, dp_bits = list(bits_of("seq")), list(bits_of("dp"))

    def own_columns(array, axis):
        return jnp.concatenate(
            [
                lax.dynamic_slice_in_dim(array, place_in_seq * mixer_columns, mixer_columns, axis),
                lax.dynamic_slice_in_dim(array, late + place_in_seq * feed_columns, feed_columns, axis),
            ],
            axis=axis,
        )

    first_image = jnp.clip(segment[0] - BEFORE, 0, images - WIN)
    top = seq_bits[-1]
    first_of_top = lax.ppermute(first_image, "seq", partners("seq", top))
    marker = segment + 1
    low_marks = lax.ppermute(jnp.append(marker[row_count - MAXLEN :], first_image), "seq", onward)
    high_marks = lax.ppermute(jnp.append(marker[:MAXLEN], first_image), "seq", back)
    low_rows = lax.ppermute(token_rows[row_count - MAXLEN :], "seq", onward)
    high_rows = lax.ppermute(token_rows[:MAXLEN], "seq", back)
    first_of_next = jnp.where(place_in_seq % 2 == 0, high_marks[MAXLEN], low_marks[MAXLEN])
    piece = own_columns(modulation_weight, 1)
    piece_far = lax.ppermute(piece, "dp", partners("dp", 2))
    piece = jnp.concatenate([piece, piece_far])
    piece = jnp.concatenate([piece, lax.ppermute(piece, "dp", partners("dp", 1))])
    turned = [lax.dynamic_slice_in_dim(cond_act, (own ^ index) * share_rows, share_rows, 1) for index in (0, 2, 1, 3)]
    product = jnp.dot(jnp.concatenate(turned, axis=1), piece, preferred_element_type=F32)
    product += row(own_columns(modulation_bias, 0))
    product = doubled(product[None], "seq", seq_bits[:-1])
    for early in (low_rows, high_rows, first_of_next.astype(F32)[None], first_of_top.astype(F32)[None]):
        product = gate(product, early)
    mine = lax.dynamic_slice_in_dim(product, first_image, WIN, 1)
    other = lax.ppermute(lax.dynamic_slice_in_dim(product, first_of_top, WIN, 1), "seq", partners("seq", top))
    upper = place_in_seq // top
    windows = jnp.concatenate([jnp.where(upper == 0, mine, other), jnp.where(upper == 0, other, mine)])
    mixer_parts = three_terms(windows[:, :, :mixer_columns].swapaxes(0, 1).reshape(WIN, -1))
    feed_parts = three_terms(windows[:, :, mixer_columns:].swapaxes(0, 1).reshape(WIN, -1))
    marks = mark_windows(marker, low_marks[:MAXLEN], high_marks[:MAXLEN])
    wide_rows = jnp.concatenate([token_rows, low_rows, high_rows])
    wide_segment = jnp.concatenate([segment, low_marks[:MAXLEN] - 1, high_marks[:MAXLEN] - 1])
    image_select = (wide_segment - first_image)[:, None] == jnp.arange(WIN, dtype=jnp.int32)[None, :]
    select = jnp.concatenate(
        [image_select, image_select, image_select, jnp.zeros((wide_segment.shape[0], TERMS - 3 * WIN), bool)], axis=1
    ).astype(BF)
    gather = jnp.concatenate(
        [image_select[:row_count].T, jnp.zeros((WIN_PAD - WIN, row_count), bool)], axis=0
    ).astype(BF)

    input_attn, queries, key_value = project(
        input_full, row_count, wide_rows, select, mixer_parts, row(query_value_bias)
    )
    output_near = lax.ppermute(output_weight, "dp", partners("dp", 1))
    output_far = lax.ppermute(output_weight, "dp", partners("dp", 2))
    output_pieces = [output_weight, output_near, output_far, lax.ppermute(output_far, "dp", partners("dp", 1))]
    output_at = (jnp.stack([own ^ index for index in range(4)]) * (share_rows // 16)).astype(jnp.int32)
    acts = [cond_act] + [lax.ppermute(gate(cond_act, input_attn), "dp", partners("dp", mask)) for mask in (1, 2, 3)]
    own_slice = lax.dynamic_slice_in_dim(modulation_weight, place_in_seq * columns, columns, 1)
    slice_full = lax.all_gather(own_slice, "dp", axis=0, tiled=True)

    attend, attend_back = attention_calls(row_count, width)
    attn_mixed, row_peaks = attend(queries, key_value, marks, ())

    attn_out, middle, input_feed, grad_feed = enter_feed(
        output_at, output_pieces, attn_mixed, token_rows, grad_out, select, feed_parts, row(output_bias),
        (),
    )
    feed_out, grad_input_feed, expand_grad, contract_grad, expand_sums, feed_sums = feed(
        seq_count, input_feed, grad_feed, expand_full, contract_full, row(expand_bias)
    )
    contract_rest = scattered(contract_grad)
    expand_rest = scattered(expand_grad)
    layer_out, grad_middle, grad_attn, grad_mixed, feed_images, attn_sums = leave_feed(
        output_at, output_pieces, feed_out, grad_input_feed, middle, attn_out, grad_out, select, gather,
        feed_parts, row(contract_bias), (*acts[1:], slice_full),
    )
    grad_query_edge, rim_low, rim_high, grad_edge = attend_back(
        True, queries, attn_mixed, grad_mixed, row_peaks, key_value, marks
    )
    from_next = lax.ppermute(rim_low, "seq", back)
    from_prev = lax.ppermute(rim_high, "seq", onward)
    grad_query, own_grad = attend_back(
        False, queries, attn_mixed, grad_mixed, row_peaks, key_value,
        marks, (grad_edge, grad_query_edge), (contract_rest,),
    )
    rims = jnp.pad(from_prev.astype(F32), ((0, row_count - MAXLEN), (0, 0))) + jnp.pad(
        from_next.astype(F32), ((row_count - MAXLEN, 0), (0, 0))
    )
    grad_pair = (own_grad + rims).astype(BF)
    contract_stages = along_rest(contract_rest)
    total_contract = contract_stages[-1][0]
    total_expand = along_rest(expand_rest)[-1][0]
    input_grad = weight_grad(
        seq_count, input_attn, grad_query, grad_pair, attn_mixed, grad_attn, (contract_stages[0],)
    )
    input_rest = scattered(input_grad)
    grad_rows, all_images, packed_sums = leave(
        input_full, grad_query, grad_pair, token_rows, grad_middle, select, gather, mixer_parts, feed_images,
        (input_grad,),
    )
    input_total = along_rest(input_rest)[-1][0]
    input_width = 3 * width // seq_count
    total_input, total_output = input_total[:, :input_width], input_total[:, input_width:]

    window_grads = all_images[:WIN]
    sums = [
        jnp.sum(window_grads, axis=0),
        jnp.sum(packed_sums, axis=0),
        jnp.sum(attn_sums, axis=0),
        jnp.sum(expand_sums, axis=0),
        jnp.sum(feed_sums, axis=0),
    ]
    ends = [sum(part.shape[0] for part in sums[: index + 1]) for index in range(5)]
    biases = jnp.concatenate(sums + [jnp.zeros((-ends[-1] % columns,), F32)]).reshape(-1, columns)
    bias_rows = biases.shape[0]

    def joined(value, axis, bit):
        high = lax.reduce_precision(biases, 8, 7)
        low = lax.reduce_precision(biases - high, 8, 7)
        got = swapped(jnp.concatenate([value.reshape(-1, columns), high, low]), axis, bit)
        rest = high + low + (wide(got[-2 * bias_rows : -bias_rows]) + wide(got[-bias_rows:]))
        return wide(got[: -2 * bias_rows]).reshape(value.shape), rest

    window_blocks = window_grads.reshape(WIN, -1, 2, columns)
    mine = lax.dynamic_index_in_dim(window_blocks, place_in_seq % 2, 2, keepdims=False)
    sent = lax.dynamic_index_in_dim(window_blocks, 1 - place_in_seq % 2, 2, keepdims=False)
    got, biases = joined(sent.swapaxes(0, 1), "seq", 1)
    empty = jnp.zeros((seq_count // 2, images, columns), F32)
    column_grads = lax.dynamic_update_slice_in_dim(empty, mine.swapaxes(0, 1), first_image, 1)
    column_grads += lax.dynamic_update_slice_in_dim(empty, got, first_of_next, 1)
    for bit in seq_bits[1:]:
        pairs = column_grads.reshape(-1, 2, images, columns)
        mine = (place_in_seq // bit) % 2
        got, biases = joined(lax.dynamic_index_in_dim(pairs, 1 - mine, 1, keepdims=False), "seq", bit)
        column_grads = lax.dynamic_index_in_dim(pairs, mine, 1, keepdims=False) + got
    column_grads = column_grads[0]
    all_grads = column_grads[None].astype(BF)
    for bit in dp_bits:
        other, biases = joined(all_grads, "dp", bit)
        other = other.astype(BF)
        mine = (own // bit) % 2
        all_grads = jnp.concatenate([jnp.where(mine == 0, all_grads, other), jnp.where(mine == 0, other, all_grads)])
    all_grads = all_grads.reshape(-1, columns)
    acts = jnp.stack([lax.dynamic_slice_in_dim(act, own * share_rows, share_rows, 1) for act in acts])
    acts = [lax.dynamic_index_in_dim(acts, own ^ index, 0, keepdims=False) for index in range(4)]
    all_act = jnp.concatenate(acts)
    total_modulation = dot_turned(all_act, all_grads)
    grad_act = lax.dot_general(
        column_grads, slice_full.astype(F32), (((1,), (1,)), ((), ())), precision=lax.Precision.HIGHEST
    )
    grad_condition = silu_back(grad_act)[0].reshape(seq_count, -1, width)
    for bit in seq_bits:
        pairs = grad_condition.reshape(-1, 2, *grad_condition.shape[1:])
        mine = (place_in_seq // bit) % 2
        got = swapped(lax.dynamic_index_in_dim(pairs, 1 - mine, 1, keepdims=False), "seq", bit, F32)
        grad_condition = lax.dynamic_index_in_dim(pairs, mine, 1, keepdims=False) + got
    grad_condition = grad_condition[0]
    bias_modulation, bias_query_value, bias_output, bias_expand, bias_contract, _ = jnp.split(
        biases.reshape(-1), ends
    )
    return (
        layer_out[None],
        grad_rows[None],
        grad_condition[None],
        total_modulation,
        bias_modulation,
        total_input,
        bias_query_value,
        total_output,
        bias_output,
        total_expand,
        bias_expand,
        total_contract.T,
        bias_contract,
    )


def solution(mesh):
    in_specs = (
        P("dp", "seq", None),
        P("dp", "seq"),
        P("dp", None, None),
        P("dp", "seq", None),
        P("dp", None),
        P(),
        P("dp", None),
        P(),
        P("dp", None),
        P(),
        P("dp", None),
        P(),
        P("dp", None),
        P(),
    )
    out_specs = (
        P("dp", "seq", None),
        P("dp", "seq", None),
        P("dp", "seq", None),
        P("dp", "seq"),
        P(),
        P("dp", "seq"),
        P(),
        P("dp", "seq"),
        P(),
        P("dp", "seq"),
        P(),
        P("dp", "seq"),
        P(),
    )
    return jax.shard_map(shards, mesh=mesh, in_specs=in_specs, out_specs=out_specs, check_vma=False)
```

```python
import functools
import math

import jax
import jax.numpy as jnp
from jax import lax
from jax.experimental import pallas as pl
from jax.experimental.pallas import tpu as pltpu
from jax.sharding import PartitionSpec as P

WIN = 24
WIN_PAD = 32
BEFORE = 3
TERMS = 128
HEADS = 16
MAXLEN = 192
HEAD = 72
BLOCK = 256
SPAN = BLOCK + 2 * MAXLEN
CHUNK = 128
STRIP = 320
STRIP_BACK = 640
BF, F32 = jnp.bfloat16, jnp.float32
SCORE_SCALE = 1.0 / math.sqrt(HEAD)
LOG2E = 1.4426950408889634
VMEM = 60 * 1024 * 1024


def dot_rows(left, right):
    return lax.dot_general(left, right, (((1,), (1,)), ((), ())), preferred_element_type=F32)


def dot_plain(left, right):
    return jnp.dot(left, right, preferred_element_type=F32)


def fill_mask(key_mark_ref, query_mark_ref, bias):
    marks = jnp.broadcast_to(key_mark_ref[0].astype(F32), (CHUNK, SPAN))
    columns = marks.T
    query = query_mark_ref[0].astype(F32)
    for lane in range(0, BLOCK, CHUNK):
        bias[:, lane : lane + CHUNK] = jnp.where(
            columns == query[:, lane : lane + CHUNK], 0.0, -1e30
        )


def head_lanes(head, width):
    first = jnp.minimum((head * HEAD) // 128 * 128, width - 256)
    lanes = lax.broadcasted_iota(jnp.int32, (1, 256), 1) + first
    inside = (lanes >= head * HEAD) & (lanes < (head + 1) * HEAD)
    return pl.multiple_of(first, 128), inside


def masked(ref, first, inside):
    block = ref[:, pl.ds(first, 256)]
    return jnp.where(inside, block, jnp.zeros_like(block))


def fill_window(block, last, pair_ref, window):
    rows = pair_ref.shape[0] - 2 * MAXLEN
    inner = SPAN - MAXLEN

    @pl.when(block == 0)
    def _():
        window[0:MAXLEN, :] = pair_ref[rows : rows + MAXLEN, :]
        window[MAXLEN:SPAN, :] = pair_ref[0:inner, :]

    @pl.when((block > 0) & (block < last))
    def _():
        window[...] = pair_ref[pl.ds(pl.multiple_of(block * BLOCK - MAXLEN, 64), SPAN), :]

    @pl.when(block == last)
    def _():
        window[0:inner, :] = pair_ref[rows - inner : rows, :]
        window[inner:SPAN, :] = pair_ref[rows + MAXLEN : rows + 2 * MAXLEN, :]


def forward_kernel(query_ref, pair_ref, key_mark_ref, query_mark_ref,
                   out_ref, peak_ref, bias, turned, scores, weights, mixed, view):
    width = query_ref.shape[1]
    fill_window(pl.program_id(0), pl.num_programs(0) - 1, pair_ref, view)
    fill_mask(key_mark_ref, query_mark_ref, bias)
    turned[...] = view[:, width : 2 * width].T
    factor = SCORE_SCALE * LOG2E

    def pair(index, carry):
        for odd in range(2):
            head = 2 * index + odd
            first, inside = head_lanes(head, width)
            query = masked(query_ref, first, inside)
            peak = jnp.full((8, BLOCK), -3e38, F32)
            for start in range(0, SPAN, STRIP):
                rows = slice(start, start + STRIP)
                score = dot_rows(view[rows, pl.ds(first, 256)], query) * factor + bias[rows, :]
                scores[odd, rows, :] = score
                peak = jnp.maximum(peak, jnp.max(score.reshape(STRIP // 8, 8, BLOCK), axis=0))
            peak = jnp.max(peak, axis=0, keepdims=True)
            total = jnp.zeros((8, BLOCK), F32)
            for start in range(0, SPAN, CHUNK):
                rows = slice(start, start + CHUNK)
                power = jnp.exp2(scores[odd, rows, :] - peak)
                total = total + jnp.sum(power.reshape(CHUNK // 8, 8, BLOCK), axis=0)
                weights[odd, rows, :] = power.astype(BF)
            total = jnp.sum(total, axis=0, keepdims=True)
            base = pl.multiple_of(index * 2 * HEAD, 16)
            value = turned[pl.ds(pl.multiple_of(base + 64 * odd, 16), 80), :]
            part = dot_plain(value, weights[odd]) * (1.0 / total)
            mixed[pl.ds(pl.multiple_of(base + HEAD * odd, 8), HEAD), :] = part[8 * odd : 8 * odd + HEAD]
            peak_ref[pl.ds(head, 1), :] = peak + jnp.log2(total)
        return carry

    lax.fori_loop(0, HEADS // 2, pair, 0)
    out_ref[...] = mixed[...].T.astype(BF)


def backward_kernel(edge, *refs):
    if edge:
        (query_ref, out_ref, grad_ref, peak_ref, pair_ref, key_mark_ref, query_mark_ref,
         grad_query_ref, rim_low_ref, rim_high_ref, grad_own_ref,
         bias, turned, weights, signals, mixed, delta, view, total) = refs
    else:
        (query_ref, out_ref, grad_ref, peak_ref, pair_ref, key_mark_ref, query_mark_ref, edge_ref, _,
         grad_query_ref, grad_own_ref,
         bias, turned, weights, signals, mixed, delta, view, sem) = refs
    width = query_ref.shape[1]
    step = pl.program_id(0)
    last = (pair_ref.shape[0] - 2 * MAXLEN) // BLOCK - 1
    fill_window(step * last if edge else step + 1, last, pair_ref, view)
    inner = SPAN - MAXLEN
    if edge:
        total[...] = jnp.zeros_like(total)
        sums = total
    else:
        rows = grad_own_ref.shape[0]

        @pl.when(step == 0)
        def _():
            low = pltpu.make_async_copy(edge_ref.at[0], grad_own_ref.at[pl.ds(0, inner)], sem.at[0])
            high = pltpu.make_async_copy(
                edge_ref.at[1], grad_own_ref.at[pl.ds(rows - inner, inner)], sem.at[1]
            )
            low.start()
            high.start()
            grad_own_ref[inner : rows - inner, :] = jnp.zeros((rows - 2 * inner, 2 * width), F32)
            low.wait()
            high.wait()

        sums = grad_own_ref.at[pl.ds(pl.multiple_of(step * BLOCK + BLOCK - MAXLEN, 64), SPAN)]
    fill_mask(key_mark_ref, query_mark_ref, bias)
    turned[...] = view[:, 0:width].T
    product = out_ref[...].astype(F32) * grad_ref[...].astype(F32)
    high = product.astype(BF)
    low = (product - high.astype(F32)).astype(BF)
    of_head = (
        lax.broadcasted_iota(jnp.int32, (HEADS, width), 1) // HEAD
        == lax.broadcasted_iota(jnp.int32, (HEADS, width), 0)
    ).astype(BF)
    delta[...] = dot_rows(of_head, high) + dot_rows(of_head, low)
    factor = SCORE_SCALE * LOG2E

    def pair(index, carry):
        for odd in range(2):
            head = 2 * index + odd
            first, inside = head_lanes(head, width)
            query = masked(query_ref, first, inside)
            grad = masked(grad_ref, first, inside)
            peak = peak_ref[pl.ds(head, 1), :]
            mean = delta[pl.ds(head, 1), :]
            for start in range(0, SPAN, STRIP_BACK):
                rows = slice(start, start + STRIP_BACK)
                score = dot_rows(view[rows, pl.ds(first, 256)], query) * factor
                power = jnp.exp2(score + (bias[rows, :] - peak))
                slope = dot_rows(view[rows, pl.ds(first + width, 256)], grad)
                low = power.astype(BF)
                signal = (power * (slope - mean)).astype(BF)
                signals[odd, rows, :] = signal
                sums[rows, pl.ds(first, 256)] += dot_plain(signal, query)
                sums[rows, pl.ds(first + width, 256)] += dot_plain(low, grad)
            base = pl.multiple_of(index * 2 * HEAD, 16)
            key = turned[pl.ds(pl.multiple_of(base + 64 * odd, 16), 80), :]
            part = dot_plain(key, signals[odd]) * SCORE_SCALE
            mixed[pl.ds(pl.multiple_of(base + HEAD * odd, 8), HEAD), :] = part[8 * odd : 8 * odd + HEAD]
        return carry

    lax.fori_loop(0, HEADS // 2, pair, 0)
    grad_query_ref[...] = mixed[...].T.astype(BF)
    if edge:

        @pl.when(step == 0)
        def _():
            rim_low_ref[:, :width] = (total[0:MAXLEN, :width] * SCORE_SCALE).astype(BF)
            rim_low_ref[:, width:] = total[0:MAXLEN, width:].astype(BF)
            grad_own_ref[0] = total[MAXLEN:SPAN, :]

        @pl.when(step == 1)
        def _():
            rim_high_ref[:, :width] = (total[inner:SPAN, :width] * SCORE_SCALE).astype(BF)
            rim_high_ref[:, width:] = total[inner:SPAN, width:].astype(BF)
            grad_own_ref[0] = total[0:inner, :]
    else:

        @pl.when(step == pl.num_programs(0) - 1)
        def _():
            grad_own_ref[:, :width] = grad_own_ref[:, :width] * SCORE_SCALE


def mark_windows(marker, marker_prev, marker_next):
    wide = jnp.concatenate([marker_prev, marker, marker_next])
    count = marker.shape[0] // BLOCK
    keys = jnp.stack([wide[i * BLOCK : i * BLOCK + SPAN] for i in range(count)])[:, None, :]
    return keys, marker.reshape(count, 1, BLOCK)


def whole(shape):
    return pl.BlockSpec(shape, lambda i: (0,) * len(shape))


def attention_calls(rows, width):
    count = rows // BLOCK
    last = count - 1
    inner = SPAN - MAXLEN
    scratch = [
        pltpu.VMEM((SPAN, BLOCK), F32),
        pltpu.VMEM((width, SPAN), BF),
    ]
    elements = SPAN * BLOCK * HEADS

    def block_specs(at):
        row_block = pl.BlockSpec((BLOCK, width), lambda i: (at(i), 0))
        lane_block = pl.BlockSpec((HEADS, BLOCK), lambda i: (0, at(i)))
        key_mark = pl.BlockSpec((1, 1, SPAN), lambda i: (at(i), 0, 0))
        query_mark = pl.BlockSpec((1, 1, BLOCK), lambda i: (at(i), 0, 0))
        return row_block, lane_block, key_mark, query_mark

    any_spec = pl.BlockSpec(memory_space=pl.ANY)
    params = pltpu.CompilerParams(vmem_limit_bytes=VMEM, dimension_semantics=("arbitrary",))
    pairs = once((rows + 2 * MAXLEN, 2 * width))
    view = pltpu.VMEM((SPAN, 2 * width), BF)

    def forward(queries, key_value, marks, after):
        row_block, lane_block, key_mark, query_mark = block_specs(lambda i: i)
        return pl.pallas_call(
            skipping(forward_kernel, 4, len(after)),
            grid=(count,),
            in_specs=[row_block, pairs, key_mark, query_mark] + [any_spec] * len(after),
            out_specs=[row_block, lane_block],
            out_shape=[
                jax.ShapeDtypeStruct((rows, width), BF),
                jax.ShapeDtypeStruct((HEADS, rows), F32),
            ],
            scratch_shapes=scratch
            + [
                pltpu.VMEM((2, SPAN, BLOCK), F32),
                pltpu.VMEM((2, SPAN, BLOCK), BF),
                pltpu.VMEM((width, BLOCK), F32),
                view,
            ],
            compiler_params=params,
            cost_estimate=cost(11.5 * count),
            name="attend",
        )(queries, key_value, *marks, *after)

    def backward(edge, queries, mixed, grad, peaks, key_value, marks, before=(), after=()):
        row_block, lane_block, key_mark, query_mark = block_specs(
            (lambda i: i * last) if edge else (lambda i: i + 1)
        )
        steps = 2 if edge else count - 2
        in_specs = [row_block, row_block, row_block, lane_block, pairs]
        in_specs += [key_mark, query_mark] + [any_spec] * (len(before) + len(after))
        rim = jax.ShapeDtypeStruct((MAXLEN, 2 * width), BF)
        if edge:
            out_specs = [row_block, whole(rim.shape), whole(rim.shape),
                         pl.BlockSpec((1, inner, 2 * width), lambda i: (i, 0, 0))]
            out_shape = [jax.ShapeDtypeStruct((rows, width), BF), rim, rim,
                         jax.ShapeDtypeStruct((2, inner, 2 * width), F32)]
            extra = [view, pltpu.VMEM((SPAN, 2 * width), F32)]
        else:
            out_specs = [row_block, whole((rows, 2 * width))]
            out_shape = [jax.ShapeDtypeStruct((rows, width), BF),
                         jax.ShapeDtypeStruct((rows, 2 * width), F32)]
            extra = [view, pltpu.SemaphoreType.DMA((2,))]
        return pl.pallas_call(
            skipping(functools.partial(backward_kernel, edge), 7 + len(before), len(after)),
            grid=(steps,),
            in_specs=in_specs,
            out_specs=out_specs,
            out_shape=out_shape,
            scratch_shapes=scratch
            + [
                pltpu.VMEM((2, SPAN, BLOCK), BF),
                pltpu.VMEM((2, SPAN, BLOCK), BF),
                pltpu.VMEM((width, BLOCK), F32),
                pltpu.VMEM((HEADS, BLOCK), F32),
            ]
            + extra,
            input_output_aliases={} if edge else {8: 0},
            compiler_params=params,
            cost_estimate=cost(2.2 * steps),
            name="attend_back_edge" if edge else "attend_back_inner",
        )(queries, mixed, grad, peaks, key_value, *marks, *before, *after)

    return forward, backward


BANDS = 4
FEED_ROWS = 512
EPSILON = 1e-06
ROOT = math.sqrt(2.0 / math.pi)
CUBE = 0.044715


def skipping(kernel, first, count):
    return lambda *refs: kernel(*refs[:first], *refs[first + count :])


def once(shape):
    return pl.BlockSpec(shape, lambda i, *_: (0,) * len(shape), pipeline_mode=pl.Buffered(buffer_count=1))


def rows_of(rows, width):
    return pl.BlockSpec((rows, width), lambda i, *_: (i, 0))


def kernel_params():
    return pltpu.CompilerParams(vmem_limit_bytes=VMEM, dimension_semantics=("arbitrary",))


def cost(microseconds):
    return pl.CostEstimate(flops=int(microseconds * 1.1e9), bytes_accessed=int(microseconds * 3e6), transcendentals=0)


def dot_turned(left, right):
    return lax.dot_general(left, right, (((0,), (0,)), ((), ())), preferred_element_type=F32)


def spread(select, parts_ref, part, width):
    return dot_plain(select, parts_ref[:, part * width : (part + 1) * width])


def normalise(block):
    centred = block - jnp.mean(block, axis=-1, keepdims=True)
    inverse = lax.rsqrt(jnp.mean(centred * centred, axis=-1, keepdims=True) + EPSILON)
    return centred * inverse, inverse


def norm_back(upstream, normed, inverse):
    return inverse * (
        upstream
        - jnp.mean(upstream, axis=-1, keepdims=True)
        - normed * jnp.mean(upstream * normed, axis=-1, keepdims=True)
    )


def image_sum(gather, block):
    high = block.astype(BF)
    low = (block - high.astype(F32)).astype(BF)
    return dot_plain(gather, high) + dot_plain(gather, low)


def column_sum(block):
    rows, width = block.shape
    return jnp.sum(block.reshape(rows // 8, 8, width), axis=0)


def piece_copies(place_ref, piece_refs, full, sems):
    copies = []
    for index, piece in enumerate(piece_refs):
        rows = piece.shape[0]
        start = pl.multiple_of(place_ref[index] * 16, 16)
        copies.append(pltpu.make_async_copy(piece, full.at[pl.ds(start, rows)], sems.at[index]))
    return copies


def begin_pieces(place_ref, piece_refs, full, sems):
    @pl.when(pl.program_id(0) == 0)
    def _():
        for copy in piece_copies(place_ref, piece_refs, full, sems):
            copy.start()


def end_pieces(place_ref, piece_refs, full, sems):
    @pl.when(pl.program_id(0) == 0)
    def _():
        for copy in piece_copies(place_ref, piece_refs, full, sems):
            copy.wait()


def project_kernel(own_rows, tokens_ref, select_ref, parts_ref, bias_ref, weight_ref, input_ref, query_ref, pair_ref):
    width = tokens_ref.shape[1]
    select = select_ref[...]
    normed, _ = normalise(tokens_ref[...].astype(F32))
    shift = spread(select, parts_ref, 0, width)
    scale = spread(select, parts_ref, 1, width)
    rows = (normed * (1.0 + scale) + shift).astype(BF)
    input_ref[...] = rows

    @pl.when(pl.program_id(0) * tokens_ref.shape[0] < own_rows)
    def _():
        query_ref[...] = (dot_plain(rows, weight_ref[:, :width]) + bias_ref[:, :width]).astype(BF)

    pair_ref[:, :width] = dot_plain(rows, weight_ref[:, width : 2 * width]).astype(BF)
    pair_ref[:, width:] = (dot_plain(rows, weight_ref[:, 2 * width :]) + bias_ref[:, width:]).astype(BF)


def project(weight, own_rows, tokens, select, parts, bias):
    rows, width = tokens.shape
    band = rows // BANDS
    return pl.pallas_call(
        functools.partial(project_kernel, own_rows),
        grid=(BANDS,),
        in_specs=[
            rows_of(band, width),
            rows_of(band, select.shape[1]),
            once(parts.shape),
            once(bias.shape),
            once(weight.shape),
        ],
        out_specs=[rows_of(band, width), rows_of(band, width), rows_of(band, 2 * width)],
        out_shape=[
            jax.ShapeDtypeStruct((rows, width), BF),
            jax.ShapeDtypeStruct((rows, width), BF),
            jax.ShapeDtypeStruct((rows, 2 * width), BF),
        ],
        compiler_params=kernel_params(),
        cost_estimate=cost(25),
        name="project",
    )(tokens, select, parts, bias, weight)


def enter_feed_kernel(count, place_ref, mixed_ref, tokens_ref, cotangent_ref, select_ref, parts_ref, bias_ref, *refs):
    pieces = refs[:count]
    attn_ref, middle_ref, input_ref, grad_feed_ref, full, sems = refs[count:]
    width = tokens_ref.shape[1]
    begin_pieces(place_ref, pieces, full, sems)
    select = select_ref[...]
    gate_mixer = spread(select, parts_ref, 0, width)
    shift = spread(select, parts_ref, 1, width)
    scale = spread(select, parts_ref, 2, width)
    gate_feed = spread(select, parts_ref, 3, width)
    grad_feed_ref[...] = (cotangent_ref[...].astype(F32) * gate_feed).astype(BF)
    end_pieces(place_ref, pieces, full, sems)
    attn = dot_plain(mixed_ref[...], full[...]) + bias_ref[...]
    attn_ref[...] = attn
    middle = tokens_ref[...].astype(F32) + gate_mixer * attn
    middle_ref[...] = middle
    normed, _ = normalise(middle)
    input_ref[...] = (normed * (1.0 + scale) + shift).astype(BF)


def enter_feed(place, pieces, mixed, tokens, cotangent, select, parts, bias, after):
    rows, width = tokens.shape
    band = rows // BANDS
    any_spec = pl.BlockSpec(memory_space=pl.ANY)
    block = rows_of(band, width)
    return pl.pallas_call(
        skipping(functools.partial(enter_feed_kernel, len(pieces)), 7 + len(pieces), len(after)),
        grid_spec=pltpu.PrefetchScalarGridSpec(
            num_scalar_prefetch=1,
            grid=(BANDS,),
            in_specs=[block, block, block, rows_of(band, select.shape[1]), once(parts.shape), once(bias.shape)]
            + [any_spec] * (len(pieces) + len(after)),
            out_specs=[block] * 4,
            scratch_shapes=[pltpu.VMEM((width, width), BF), pltpu.SemaphoreType.DMA((len(pieces),))],
        ),
        out_shape=[jax.ShapeDtypeStruct((rows, width), kind) for kind in (F32, F32, BF, BF)],
        compiler_params=kernel_params(),
        cost_estimate=cost(14),
        name="enter_feed",
    )(place, mixed, tokens, cotangent, select, parts, bias, *pieces, *after)


def feed_kernel(later, place_ref, input_ref, grad_ref, expand_ref, bias_ref, *refs):
    if later:
        contract_ref, before_out_ref, before_grad_ref = refs[:3]
        refs = refs[7:]
    else:
        own_ref, near_ref = refs[:2]
        held, sems = refs[-2:]
        refs = refs[2:-2]
        before_out_ref = before_grad_ref = None
        step = pl.program_id(0)
        own_copy = pltpu.make_async_copy(own_ref, held.at[0], sems.at[0])
        near_copy = pltpu.make_async_copy(near_ref, held.at[1], sems.at[1])

        @pl.when(step == 0)
        def _():
            own_copy.start()
            near_copy.start()
            own_copy.wait()

        @pl.when(step == 1)
        def _():
            near_copy.wait()

        contract_ref = held.at[step]
    feed_step(place_ref, input_ref, grad_ref, expand_ref, contract_ref, bias_ref, before_out_ref, before_grad_ref, *refs)


def feed_step(place_ref, input_ref, grad_ref, expand_ref, contract_ref, bias_ref, before_out_ref, before_grad_ref,
                out_ref, grad_input_ref, keep_ref, send_ref, contract_grad_ref, bias_grad_ref, grad_sum_ref,
                input_turned, grad_turned, active, hidden_grad):
    step = pl.program_id(0)
    rows, width = input_ref.shape

    @pl.when(step == 0)
    def _():
        input_turned[...] = input_ref[...].T
        grad_turned[...] = grad_ref[...].T
        grad_sum_ref[...] = column_sum(grad_ref[...].astype(F32))
        if before_out_ref is None:
            out_ref[...] = jnp.zeros_like(out_ref)
            grad_input_ref[...] = jnp.zeros_like(grad_input_ref)
        else:
            out_ref[...] = before_out_ref[...]
            grad_input_ref[...] = before_grad_ref[...]

    bias_grad_ref[...] = jnp.zeros_like(bias_grad_ref)

    def band(index, carry):
        here = pl.ds(pl.multiple_of(index * FEED_ROWS, FEED_ROWS), FEED_ROWS)
        hidden = dot_plain(input_ref[here, :], expand_ref[...]) + bias_ref[...]
        square = hidden * hidden
        bent = jnp.tanh(ROOT * hidden * (1.0 + CUBE * square))
        half = 0.5 + 0.5 * bent
        active[here, :] = (hidden * half).astype(BF)
        slope = half + (0.5 * ROOT) * hidden * (1.0 - bent * bent) * (1.0 + (3.0 * CUBE) * square)
        pulled = dot_rows(grad_ref[here, :], contract_ref[...])
        low = (pulled * slope).astype(BF)
        hidden_grad[here, :] = low
        bias_grad_ref[...] += column_sum(low.astype(F32))
        out_ref[here, :] += dot_plain(active[here, :], contract_ref[...])
        grad_input_ref[here, :] += dot_rows(low, expand_ref[...])
        return carry

    lax.fori_loop(0, rows // FEED_ROWS, band, 0)
    share = width // 4
    block = keep_ref.shape[4]
    for index in range(4):
        start = pl.multiple_of(place_ref[index] * 16, 16)
        part = dot_plain(input_turned[pl.ds(start, share), :], hidden_grad[...]).astype(BF)
        store_owners(send_ref if index % 2 else keep_ref, place_ref[4 + index], part, 0, block, 0)
    for index in range(4):
        here = slice(index * share, (index + 1) * share)
        part = dot_plain(grad_turned[here, :], active[...]).astype(BF)
        if len(contract_grad_ref.shape) == 3:
            contract_grad_ref[0, here, :] = part
        else:
            rows = contract_grad_ref.shape[3]
            for start in range(0, share, rows):
                rest, side = divmod((index * share + start) // rows, 2)
                contract_grad_ref[0, side, rest] = part[start : start + rows]


def feed(place, seq_count, inputs, grad_feed, expand, contracts, bias, before=()):
    rows, width = inputs.shape
    hidden = expand.shape[1]
    quarters = hidden // width
    whole_rows = once((rows, width))
    rest = seq_count // 2
    expand_shape = (2, 2, rest, width // 4, hidden // seq_count)
    expand_block = pl.BlockSpec((2, 2, rest // quarters) + expand_shape[3:], lambda i, place: (0, 0, place[8 + i], 0, 0))
    if width // seq_count % 16 == 0:
        contract_shape = (quarters, 2, rest, width // seq_count, width)
    else:
        contract_shape = (quarters, width, width)
    zeros = (0,) * (len(contract_shape) - 1)
    any_spec = pl.BlockSpec(memory_space=pl.ANY)
    result = pl.pallas_call(
        functools.partial(feed_kernel, bool(before)),
        grid_spec=pltpu.PrefetchScalarGridSpec(
            num_scalar_prefetch=1,
            grid=(quarters // 2,),
            in_specs=[
                whole_rows,
                whole_rows,
                pl.BlockSpec((width, width), lambda i, place: (0, place[8 + i])),
                pl.BlockSpec((1, width), lambda i, place: (0, place[8 + i])),
            ]
            + (
                [pl.BlockSpec((width, width), lambda i, place: (place[8 + i], 0))] + [whole_rows] * 2 + [any_spec] * 4
                if before
                else [any_spec] * 2
            ),
            out_specs=[
                whole_rows,
                whole_rows,
                expand_block,
                expand_block,
                pl.BlockSpec((1,) + contract_shape[1:], lambda i, place: (place[8 + i],) + zeros),
                pl.BlockSpec((8, width), lambda i, place: (0, place[8 + i])),
                once((8, width)),
            ],
            scratch_shapes=[
                pltpu.VMEM((width, rows), BF),
                pltpu.VMEM((width, rows), BF),
                pltpu.VMEM((rows, width), BF),
                pltpu.VMEM((rows, width), BF),
            ]
            + ([] if before else [pltpu.VMEM((2, width, width), BF), pltpu.SemaphoreType.DMA((2,))]),
        ),
        out_shape=[
            jax.ShapeDtypeStruct((rows, width), F32),
            jax.ShapeDtypeStruct((rows, width), F32),
            jax.ShapeDtypeStruct(expand_shape, BF),
            jax.ShapeDtypeStruct(expand_shape, BF),
            jax.ShapeDtypeStruct(contract_shape, BF),
            jax.ShapeDtypeStruct((8, hidden), F32),
            jax.ShapeDtypeStruct((8, width), F32),
        ],
        input_output_aliases={8: 2, 9: 3, 10: 4, 11: 5} if before else {},
        compiler_params=kernel_params(),
        cost_estimate=cost(47),
        name="feed_later" if before else "feed",
    )(place, inputs, grad_feed, expand, bias, *contracts, *before)
    return result


def leave_feed_kernel(count, place_ref, feed_ref, grad_input_ref, middle_ref, attn_ref, cotangent_ref, select_ref,
                      gather_ref, parts_ref, bias_ref, *refs):
    pieces = refs[:count]
    out_ref, grad_middle_ref, grad_attn_ref, grad_mixed_ref, image_ref, sum_ref, full, sems = refs[count:]
    width = middle_ref.shape[1]
    step = pl.program_id(0)
    begin_pieces(place_ref, pieces, full, sems)
    select = select_ref[...]
    gather = gather_ref[...]

    @pl.when(step == 0)
    def _():
        image_ref[...] = jnp.zeros_like(image_ref)
        sum_ref[...] = jnp.zeros_like(sum_ref)

    middle = middle_ref[...]
    grad_out = cotangent_ref[...].astype(F32)
    feed_out = feed_ref[...] + bias_ref[...]
    out_ref[...] = (middle + spread(select, parts_ref, 3, width) * feed_out).astype(BF)
    image_ref[:, 3 * width :] += image_sum(gather, grad_out * feed_out)
    grad_input = grad_input_ref[...]
    image_ref[:, width : 2 * width] += image_sum(gather, grad_input)
    normed, inverse = normalise(middle)
    image_ref[:, 2 * width : 3 * width] += image_sum(gather, grad_input * normed)
    scale = spread(select, parts_ref, 2, width)
    grad_middle = grad_out + norm_back(grad_input * (1.0 + scale), normed, inverse)
    grad_middle_ref[...] = grad_middle
    image_ref[:, :width] += image_sum(gather, grad_middle * attn_ref[...])
    grad_attn = (grad_middle * spread(select, parts_ref, 0, width)).astype(BF)
    grad_attn_ref[...] = grad_attn
    sum_ref[...] += column_sum(grad_attn.astype(F32))
    end_pieces(place_ref, pieces, full, sems)
    grad_mixed_ref[...] = dot_rows(grad_attn, full[...]).astype(BF)


def leave_feed(place, pieces, feed_out, grad_input, middle, attn, cotangent, select, gather, parts, bias, after):
    rows, width = middle.shape
    band = rows // BANDS
    any_spec = pl.BlockSpec(memory_space=pl.ANY)
    block = rows_of(band, width)
    images = gather.shape[0]
    return pl.pallas_call(
        skipping(functools.partial(leave_feed_kernel, len(pieces)), 10 + len(pieces), len(after)),
        grid_spec=pltpu.PrefetchScalarGridSpec(
            num_scalar_prefetch=1,
            grid=(BANDS,),
            in_specs=[block] * 5
            + [rows_of(band, select.shape[1]), pl.BlockSpec((images, band), lambda i, *_: (0, i)),
               once(parts.shape), once(bias.shape)]
            + [any_spec] * (len(pieces) + len(after)),
            out_specs=[block] * 4 + [once((images, 4 * width)), once((8, width))],
            scratch_shapes=[pltpu.VMEM((width, width), BF), pltpu.SemaphoreType.DMA((len(pieces),))],
        ),
        out_shape=[jax.ShapeDtypeStruct((rows, width), kind) for kind in (BF, F32, BF, BF)]
        + [jax.ShapeDtypeStruct((images, 4 * width), F32), jax.ShapeDtypeStruct((8, width), F32)],
        compiler_params=kernel_params(),
        cost_estimate=cost(2.2),
        name="leave_feed",
    )(place, feed_out, grad_input, middle, attn, cotangent, select, gather, parts, bias, *pieces, *after)


def store_owners(out_ref, lead, part, first, block, base):
    columns = part.shape[1]
    at = 0
    while at < columns:
        owner, offset = divmod(first + at, block)
        count = min(block - offset, columns - at)
        rest, side = divmod(owner, 2)
        out_ref[lead, side, rest, :, base + offset : base + offset + count] = part[:, at : at + count]
        at += count


def weight_grad_kernel(place_ref, input_ref, query_ref, pair_ref, mixed_ref, attn_ref, keep_ref, send_ref, turned):
    step = pl.program_id(0)
    width = query_ref.shape[1]
    share = width // 4
    block = keep_ref.shape[4] // 4

    def store(grad_ref, first, block, base):
        for index in range(4):
            start = pl.multiple_of(place_ref[index] * 16, 16)
            part = dot_plain(turned[pl.ds(start, share), :], grad_ref[...]).astype(BF)
            store_owners(send_ref if index % 2 else keep_ref, place_ref[4 + index], part, first, block, base)

    @pl.when(step == 0)
    def _():
        turned[...] = input_ref[...].T
        store(query_ref, 0, 3 * block, 0)

    for number in (1, 2):

        @pl.when(step == number)
        def _(number=number):
            store(pair_ref, number * width, 3 * block, 0)

    @pl.when(step == 3)
    def _():
        turned[...] = mixed_ref[...].T
        store(attn_ref, 0, block, 3 * block)


def weight_grad(place, seq_count, inputs, query, pair, mixed, attn, after):
    rows, width = query.shape
    shape = (2, 2, seq_count // 2, width // 4, 4 * width // seq_count)
    whole_rows = once((rows, width))
    return pl.pallas_call(
        skipping(weight_grad_kernel, 6, len(after)),
        grid_spec=pltpu.PrefetchScalarGridSpec(
        num_scalar_prefetch=1,
        grid=(4,),
        in_specs=[
            whole_rows,
            whole_rows,
            pl.BlockSpec((rows, width), lambda i, *_: (0, jnp.clip(i - 1, 0, 1))),
            whole_rows,
            whole_rows,
        ]
        + [pl.BlockSpec(memory_space=pl.ANY)] * len(after),
        out_specs=[once(shape), once(shape)],
        scratch_shapes=[pltpu.VMEM((width, rows), BF)],
        ),
        out_shape=[jax.ShapeDtypeStruct(shape, BF)] * 2,
        compiler_params=kernel_params(),
        cost_estimate=cost(2),
        name="weight_grad",
    )(place, inputs, query, pair, mixed, attn, *after)


def leave_kernel(query_ref, pair_ref, tokens_ref, grad_middle_ref, select_ref, gather_ref, parts_ref, weight_ref,
                 feed_images_ref, grad_ref, image_ref, sum_ref):
    width = tokens_ref.shape[1]
    select = select_ref[...]
    gather = gather_ref[...]

    @pl.when(pl.program_id(0) == 0)
    def _():
        image_ref[:, : 2 * width] = jnp.zeros_like(image_ref[:, : 2 * width])
        image_ref[:, 2 * width :] = feed_images_ref[...]
        sum_ref[...] = jnp.zeros_like(sum_ref)

    query = query_ref[...]
    pair = pair_ref[...]
    sum_ref[:, :width] += column_sum(query.astype(F32))
    sum_ref[:, width:] += column_sum(pair[:, width:].astype(F32))
    normed, inverse = normalise(tokens_ref[...].astype(F32))
    scale = spread(select, parts_ref, 1, width)
    grad_input = dot_rows(query, weight_ref[:, :width]) + dot_rows(pair, weight_ref[:, width:])
    image_ref[:, :width] += image_sum(gather, grad_input)
    image_ref[:, width : 2 * width] += image_sum(gather, grad_input * normed)
    grad_ref[...] = grad_middle_ref[...] + norm_back(grad_input * (1.0 + scale), normed, inverse)


def leave(weight, query, pair, tokens, grad_middle, select, gather, parts, feed_images, after):
    rows, width = tokens.shape
    band = rows // BANDS
    block = rows_of(band, width)
    images = gather.shape[0]
    return pl.pallas_call(
        skipping(leave_kernel, 9, len(after)),
        grid=(BANDS,),
        in_specs=[block, rows_of(band, 2 * width), block, block, rows_of(band, select.shape[1]),
                  pl.BlockSpec((images, band), lambda i: (0, i)), once(parts.shape), once(weight.shape),
                  once(feed_images.shape)]
        + [pl.BlockSpec(memory_space=pl.ANY)] * len(after),
        out_specs=[block, once((images, 6 * width)), once((8, 2 * width))],
        out_shape=[
            jax.ShapeDtypeStruct((rows, width), F32),
            jax.ShapeDtypeStruct((images, 6 * width), F32),
            jax.ShapeDtypeStruct((8, 2 * width), F32),
        ],
        compiler_params=kernel_params(),
        cost_estimate=cost(2.5),
        name="leave",
    )(query, pair, tokens, grad_middle, select, gather, parts, weight, feed_images, *after)


def partners(axis, bit):
    return [(i, i ^ bit) for i in range(lax.axis_size(axis))]


def bits_of(axis):
    bit = 1
    while bit < lax.axis_size(axis):
        yield bit
        bit *= 2


def doubled(value, axis, bits=None):
    place = lax.axis_index(axis)
    for bit in bits_of(axis) if bits is None else bits:
        other = lax.ppermute(value, axis, partners(axis, bit))
        mine = (place // bit) % 2
        value = jnp.concatenate([jnp.where(mine == 0, value, other), jnp.where(mine == 0, other, value)])
    return value


def neighbour_groups():
    dp_count, seq_count = lax.axis_size("dp"), lax.axis_size("seq")
    return [
        [d * seq_count + 2 * pair + side for d in range(dp_count) for side in range(2)]
        for pair in range(seq_count // 2)
    ]


def gathered(weight):
    rows = weight.shape[0] // 2
    half = lax.dynamic_slice_in_dim(weight, lax.axis_index("seq") % 2 * rows, rows, 0)
    return lax.all_gather(half, ("dp", "seq"), axis=0, tiled=True, axis_index_groups=neighbour_groups())


def scattered(grad):
    return lax.psum_scatter(
        grad.reshape(-1, *grad.shape[2:]), ("dp", "seq"), scatter_dimension=0, axis_index_groups=neighbour_groups()
    )


def scattered_core(keep, send, other):
    seq_count = lax.axis_size("seq")
    total = gate((wide(keep) + wide(swapped(send, "dp", 1))).astype(BF), other)
    groups = [
        [(2 * y + core) * seq_count + 2 * pair + side for y in range(2) for side in range(2)]
        for core in range(2)
        for pair in range(seq_count // 2)
    ]
    return total, lax.psum_scatter(
        total.reshape(-1, *total.shape[2:]), ("dp", "seq"), scatter_dimension=0, axis_index_groups=groups
    )


def along_rest(rest):
    stages = []
    for bit in list(bits_of("seq"))[1:]:
        pairs = rest.reshape(-1, 2, *rest.shape[1:])
        mine = (lax.axis_index("seq") // bit) % 2
        sent = lax.dynamic_index_in_dim(pairs, 1 - mine, 1, keepdims=False)
        rest = wide(lax.dynamic_index_in_dim(pairs, mine, 1, keepdims=False)) + wide(swapped(sent, "seq", bit))
        stages.append(rest)
    return stages


def gate(value, other):
    first = other[(0,) * other.ndim]
    return jnp.where(first == first, value, jnp.zeros_like(value))


def swapped(value, axis, bit, kind=BF):
    return lax.ppermute(value.astype(kind), axis, partners(axis, bit))


def wide(value):
    return value.astype(F32)


def split_owners(value):
    return value.reshape(2, -1, 2, *value.shape[2:])


def three_terms(value):
    high = lax.reduce_precision(value, 8, 7)
    middle = lax.reduce_precision(value - high, 8, 7)
    low = value - high - middle
    high, middle, low = high.astype(BF), middle.astype(BF), low.astype(BF)
    pad = jnp.zeros((TERMS - 3 * WIN, value.shape[1]), BF)
    return jnp.concatenate([high, middle, low, pad])


def shards(
    tokens,
    segments,
    condition,
    cotangent,
    modulation_weight,
    modulation_bias,
    input_weight,
    query_value_bias,
    output_weight,
    output_bias,
    expand_weight,
    expand_bias,
    contract_weight,
    contract_bias,
):
    token_rows = tokens[0]
    segment = segments[0]
    conditions = condition[0].astype(F32)
    grad_out = cotangent[0]
    row_count, width = token_rows.shape
    images = conditions.shape[0]
    own = lax.axis_index("dp")
    place_in_seq = lax.axis_index("seq")
    seq_count = lax.axis_size("seq")
    onward = [(i, i + 1) for i in range(seq_count - 1)]
    back = [(i + 1, i) for i in range(seq_count - 1)]
    columns = modulation_weight.shape[1] // seq_count
    row = lambda bias: bias.astype(F32)[None, :]

    input_full = gathered(input_weight)
    expand_full = gathered(expand_weight)
    contract_full = gathered(contract_weight)
    silu_all, silu_back = jax.vjp(jax.nn.silu, conditions)
    cond_act = silu_all.astype(BF)
    late = 2 * width
    mixer_columns = late // seq_count
    feed_columns = 4 * width // seq_count
    share_rows = width // 4
    seq_bits, dp_bits = list(bits_of("seq")), list(bits_of("dp"))

    def own_columns(array, axis):
        return jnp.concatenate(
            [
                lax.dynamic_slice_in_dim(array, place_in_seq * mixer_columns, mixer_columns, axis),
                lax.dynamic_slice_in_dim(array, late + place_in_seq * feed_columns, feed_columns, axis),
            ],
            axis=axis,
        )

    first_image = jnp.clip(segment[0] - BEFORE, 0, images - WIN)
    top = seq_bits[-1]
    first_of_top = lax.ppermute(first_image, "seq", partners("seq", top))
    marker = segment + 1
    low_marks = lax.ppermute(jnp.append(marker[row_count - MAXLEN :], first_image), "seq", onward)
    high_marks = lax.ppermute(jnp.append(marker[:MAXLEN], first_image), "seq", back)
    low_rows = lax.ppermute(token_rows[row_count - MAXLEN :], "seq", onward)
    high_rows = lax.ppermute(token_rows[:MAXLEN], "seq", back)
    first_of_next = jnp.where(place_in_seq % 2 == 0, high_marks[MAXLEN], low_marks[MAXLEN])
    piece = own_columns(modulation_weight, 1)
    piece_far = lax.ppermute(piece, "dp", partners("dp", 2))
    piece = jnp.concatenate([piece, piece_far])
    piece = jnp.concatenate([piece, lax.ppermute(piece, "dp", partners("dp", 1))])
    turned = [lax.dynamic_slice_in_dim(cond_act, (own ^ index) * share_rows, share_rows, 1) for index in (0, 2, 1, 3)]
    product = jnp.dot(jnp.concatenate(turned, axis=1), piece, preferred_element_type=F32)
    product += row(own_columns(modulation_bias, 0))
    product = doubled(product[None], "seq", seq_bits[:1])
    output_far = lax.ppermute(gate(output_weight, product), "dp", partners("dp", 2))
    product = doubled(product, "seq", seq_bits[1:-1])
    for early in (low_rows, high_rows, first_of_next.astype(F32)[None], first_of_top.astype(F32)[None]):
        product = gate(product, early)
    mine = lax.dynamic_slice_in_dim(product, first_image, WIN, 1)
    other = lax.ppermute(lax.dynamic_slice_in_dim(product, first_of_top, WIN, 1), "seq", partners("seq", top))
    upper = place_in_seq // top
    windows = jnp.concatenate([jnp.where(upper == 0, mine, other), jnp.where(upper == 0, other, mine)])
    mixer_parts = three_terms(windows[:, :, :mixer_columns].swapaxes(0, 1).reshape(WIN, -1))
    feed_parts = three_terms(windows[:, :, mixer_columns:].swapaxes(0, 1).reshape(WIN, -1))
    marks = mark_windows(marker, low_marks[:MAXLEN], high_marks[:MAXLEN])
    wide_rows = jnp.concatenate([token_rows, low_rows, high_rows])
    wide_segment = jnp.concatenate([segment, low_marks[:MAXLEN] - 1, high_marks[:MAXLEN] - 1])
    image_select = (wide_segment - first_image)[:, None] == jnp.arange(WIN, dtype=jnp.int32)[None, :]
    select = jnp.concatenate(
        [image_select, image_select, image_select, jnp.zeros((wide_segment.shape[0], TERMS - 3 * WIN), bool)], axis=1
    ).astype(BF)
    gather = jnp.concatenate(
        [image_select[:row_count].T, jnp.zeros((WIN_PAD - WIN, row_count), bool)], axis=0
    ).astype(BF)

    input_attn, queries, key_value = project(
        input_full, row_count, wide_rows, select, mixer_parts, row(query_value_bias)
    )
    output_near = lax.ppermute(output_weight, "dp", partners("dp", 1))
    output_pieces = [output_weight, output_near, output_far, lax.ppermute(output_far, "dp", partners("dp", 1))]
    output_at = (jnp.stack([own ^ index for index in range(4)]) * (share_rows // 16)).astype(jnp.int32)
    acts = [cond_act] + [lax.ppermute(gate(cond_act, input_attn), "dp", partners("dp", mask)) for mask in (1, 2, 3)]
    own_slice = lax.dynamic_slice_in_dim(modulation_weight, place_in_seq * columns, columns, 1)
    slice_full = lax.all_gather(own_slice, "dp", axis=0, tiled=True)

    attend, attend_back = attention_calls(row_count, width)
    attn_mixed, row_peaks = attend(queries, key_value, marks, ())

    attn_out, middle, input_feed, grad_feed = enter_feed(
        output_at, output_pieces, attn_mixed, token_rows, grad_out, select, feed_parts, row(output_bias),
        (),
    )
    chunks = jnp.stack([own ^ index for index in range(4)])
    chunks = jnp.concatenate([chunks * (share_rows // 16), chunks // 2, chunks]).astype(jnp.int32)
    contract_pair = contract_weight, lax.ppermute(contract_weight, "dp", partners("dp", 1))
    feed_before = feed(chunks[:10], seq_count, input_feed, grad_feed, expand_full, contract_pair, row(expand_bias))
    later = jnp.concatenate([chunks[:8], chunks[10:]])
    feed_out, grad_input_feed, expand_keep, expand_send, contract_grad, expand_sums, feed_sums = feed(
        later, seq_count, input_feed, grad_feed, expand_full, (contract_full,), row(expand_bias), feed_before[:6]
    )
    if len(contract_grad.shape) == 3:
        contract_grad = contract_grad.reshape(4, seq_count // 2, 2, width // seq_count, width).swapaxes(1, 2)
    contract_rest = scattered(contract_grad)
    layer_out, grad_middle, grad_attn, grad_mixed, feed_images, attn_sums = leave_feed(
        output_at, output_pieces, feed_out, grad_input_feed, middle, attn_out, grad_out, select, gather,
        feed_parts, row(contract_bias), (*acts[1:], slice_full),
    )
    expand_total, expand_rest = scattered_core(expand_keep, expand_send, grad_mixed)
    grad_query_edge, rim_low, rim_high, grad_edge = attend_back(
        True, queries, attn_mixed, grad_mixed, row_peaks, key_value, marks, (), (expand_total,)
    )
    from_next = lax.ppermute(rim_low, "seq", back)
    from_prev = lax.ppermute(rim_high, "seq", onward)
    grad_query, own_grad = attend_back(
        False, queries, attn_mixed, grad_mixed, row_peaks, key_value,
        marks, (grad_edge, grad_query_edge), (contract_rest,),
    )
    rims = jnp.pad(from_prev.astype(F32), ((0, row_count - MAXLEN), (0, 0))) + jnp.pad(
        from_next.astype(F32), ((row_count - MAXLEN, 0), (0, 0))
    )
    grad_pair = (own_grad + rims).astype(BF)
    contract_stages = along_rest(contract_rest)
    total_contract = contract_stages[-1][0]
    total_expand = along_rest(expand_rest)[-1][0]
    input_keep, input_send = weight_grad(
        chunks, seq_count, input_attn, grad_query, grad_pair, attn_mixed, grad_attn, ()
    )
    input_rest = scattered_core(input_keep, input_send, input_keep)[1]
    grad_rows, all_images, packed_sums = leave(
        input_full, grad_query, grad_pair, token_rows, grad_middle, select, gather, mixer_parts, feed_images,
        (input_send, contract_stages[0]),
    )
    input_stages = along_rest(input_rest)
    input_total = input_stages[-1][0]
    input_width = 3 * width // seq_count
    total_input, total_output = input_total[:, :input_width], input_total[:, input_width:]

    window_grads = all_images[:WIN]
    sums = [
        jnp.sum(window_grads, axis=0),
        jnp.sum(packed_sums, axis=0),
        jnp.sum(attn_sums, axis=0),
        jnp.sum(expand_sums, axis=0),
        jnp.sum(feed_sums, axis=0),
    ]
    ends = [sum(part.shape[0] for part in sums[: index + 1]) for index in range(5)]
    biases = jnp.concatenate(sums + [jnp.zeros((-ends[-1] % columns,), F32)]).reshape(-1, columns)
    bias_rows = biases.shape[0]

    def joined(value, axis, bit):
        high = lax.reduce_precision(biases, 8, 7)
        low = lax.reduce_precision(biases - high, 8, 7)
        got = swapped(jnp.concatenate([value.reshape(-1, columns), high, low]), axis, bit)
        rest = high + low + (wide(got[-2 * bias_rows : -bias_rows]) + wide(got[-bias_rows:]))
        return wide(got[: -2 * bias_rows]).reshape(value.shape), rest

    window_blocks = window_grads.reshape(WIN, -1, 2, columns)
    mine = lax.dynamic_index_in_dim(window_blocks, place_in_seq % 2, 2, keepdims=False)
    sent = lax.dynamic_index_in_dim(window_blocks, 1 - place_in_seq % 2, 2, keepdims=False)
    got, biases = joined(sent.swapaxes(0, 1), "seq", 1)
    empty = jnp.zeros((seq_count // 2, images, columns), F32)
    column_grads = lax.dynamic_update_slice_in_dim(empty, mine.swapaxes(0, 1), first_image, 1)
    column_grads += lax.dynamic_update_slice_in_dim(empty, got, first_of_next, 1)
    for bit in seq_bits[1:]:
        if bit == top:
            column_grads = gate(column_grads, input_rest)
        pairs = column_grads.reshape(-1, 2, images, columns)
        mine = (place_in_seq // bit) % 2
        got, biases = joined(lax.dynamic_index_in_dim(pairs, 1 - mine, 1, keepdims=False), "seq", bit)
        column_grads = lax.dynamic_index_in_dim(pairs, mine, 1, keepdims=False) + got
    column_grads = column_grads[0]
    all_grads = column_grads[None].astype(BF)
    for bit in dp_bits:
        other, biases = joined(all_grads, "dp", bit)
        other = other.astype(BF)
        mine = (own // bit) % 2
        all_grads = jnp.concatenate([jnp.where(mine == 0, all_grads, other), jnp.where(mine == 0, other, all_grads)])
    all_grads = all_grads.reshape(-1, columns)
    acts = jnp.stack([lax.dynamic_slice_in_dim(act, own * share_rows, share_rows, 1) for act in acts])
    acts = [lax.dynamic_index_in_dim(acts, own ^ index, 0, keepdims=False) for index in range(4)]
    all_act = jnp.concatenate(acts)
    total_modulation = dot_turned(all_act, all_grads)
    grad_act = lax.dot_general(
        column_grads, slice_full.astype(F32), (((1,), (1,)), ((), ())), precision=lax.Precision.HIGHEST
    )
    grad_condition = silu_back(grad_act)[0].reshape(seq_count, -1, width)
    for bit in seq_bits:
        if bit == seq_bits[1]:
            grad_condition = gate(grad_condition, input_stages[0])
        pairs = grad_condition.reshape(-1, 2, *grad_condition.shape[1:])
        mine = (place_in_seq // bit) % 2
        got = swapped(lax.dynamic_index_in_dim(pairs, 1 - mine, 1, keepdims=False), "seq", bit, F32)
        grad_condition = lax.dynamic_index_in_dim(pairs, mine, 1, keepdims=False) + got
    grad_condition = grad_condition[0]
    bias_modulation, bias_query_value, bias_output, bias_expand, bias_contract, _ = jnp.split(
        biases.reshape(-1), ends
    )
    return (
        layer_out[None],
        grad_rows[None],
        grad_condition[None],
        total_modulation,
        bias_modulation,
        total_input,
        bias_query_value,
        total_output,
        bias_output,
        total_expand,
        bias_expand,
        total_contract.T,
        bias_contract,
    )


def solution(mesh):
    in_specs = (
        P("dp", "seq", None),
        P("dp", "seq"),
        P("dp", None, None),
        P("dp", "seq", None),
        P("dp", None),
        P(),
        P("dp", None),
        P(),
        P("dp", None),
        P(),
        P("dp", None),
        P(),
        P("dp", None),
        P(),
    )
    out_specs = (
        P("dp", "seq", None),
        P("dp", "seq", None),
        P("dp", "seq", None),
        P("dp", "seq"),
        P(),
        P("dp", "seq"),
        P(),
        P("dp", "seq"),
        P(),
        P("dp", "seq"),
        P(),
        P("dp", "seq"),
        P(),
    )
    return jax.shard_map(shards, mesh=mesh, in_specs=in_specs, out_specs=out_specs, check_vma=False)
```

```python
import functools
import math

import jax
import jax.numpy as jnp
from jax import lax
from jax.experimental import pallas as pl
from jax.experimental.pallas import tpu as pltpu
from jax.sharding import PartitionSpec as P

WIN = 24
WIN_PAD = 32
BEFORE = 3
TERMS = 128
HEADS = 16
MAXLEN = 192
HEAD = 72
BLOCK = 256
SPAN = BLOCK + 2 * MAXLEN
CHUNK = 128
STRIP = 320
STRIP_BACK = 640
BF, F32 = jnp.bfloat16, jnp.float32
SCORE_SCALE = 1.0 / math.sqrt(HEAD)
LOG2E = 1.4426950408889634
VMEM = 60 * 1024 * 1024


def dot_rows(left, right):
    return lax.dot_general(left, right, (((1,), (1,)), ((), ())), preferred_element_type=F32)


def dot_plain(left, right):
    return jnp.dot(left, right, preferred_element_type=F32)


def fill_mask(key_mark_ref, query_mark_ref, bias):
    marks = jnp.broadcast_to(key_mark_ref[0].astype(F32), (CHUNK, SPAN))
    columns = marks.T
    query = query_mark_ref[0].astype(F32)
    for lane in range(0, BLOCK, CHUNK):
        bias[:, lane : lane + CHUNK] = jnp.where(
            columns == query[:, lane : lane + CHUNK], 0.0, -1e30
        )


def head_lanes(head, width):
    first = jnp.minimum((head * HEAD) // 128 * 128, width - 256)
    lanes = lax.broadcasted_iota(jnp.int32, (1, 256), 1) + first
    inside = (lanes >= head * HEAD) & (lanes < (head + 1) * HEAD)
    return pl.multiple_of(first, 128), inside


def masked(ref, first, inside):
    block = ref[:, pl.ds(first, 256)]
    return jnp.where(inside, block, jnp.zeros_like(block))


def fill_window(block, last, pair_ref, window):
    rows = pair_ref.shape[0] - 2 * MAXLEN
    inner = SPAN - MAXLEN

    @pl.when(block == 0)
    def _():
        window[0:MAXLEN, :] = pair_ref[rows : rows + MAXLEN, :]
        window[MAXLEN:SPAN, :] = pair_ref[0:inner, :]

    @pl.when((block > 0) & (block < last))
    def _():
        window[...] = pair_ref[pl.ds(pl.multiple_of(block * BLOCK - MAXLEN, 64), SPAN), :]

    @pl.when(block == last)
    def _():
        window[0:inner, :] = pair_ref[rows - inner : rows, :]
        window[inner:SPAN, :] = pair_ref[rows + MAXLEN : rows + 2 * MAXLEN, :]


def forward_kernel(query_ref, pair_ref, key_mark_ref, query_mark_ref,
                   out_ref, peak_ref, bias, turned, scores, weights, mixed, view):
    width = query_ref.shape[1]
    fill_window(pl.program_id(0), pl.num_programs(0) - 1, pair_ref, view)
    fill_mask(key_mark_ref, query_mark_ref, bias)
    turned[...] = view[:, width : 2 * width].T
    factor = SCORE_SCALE * LOG2E

    def pair(index, carry):
        for odd in range(2):
            head = 2 * index + odd
            first, inside = head_lanes(head, width)
            query = masked(query_ref, first, inside)
            peak = jnp.full((8, BLOCK), -3e38, F32)
            for start in range(0, SPAN, STRIP):
                rows = slice(start, start + STRIP)
                score = dot_rows(view[rows, pl.ds(first, 256)], query) * factor + bias[rows, :]
                scores[odd, rows, :] = score
                peak = jnp.maximum(peak, jnp.max(score.reshape(STRIP // 8, 8, BLOCK), axis=0))
            peak = jnp.max(peak, axis=0, keepdims=True)
            total = jnp.zeros((8, BLOCK), F32)
            for start in range(0, SPAN, CHUNK):
                rows = slice(start, start + CHUNK)
                power = jnp.exp2(scores[odd, rows, :] - peak)
                total = total + jnp.sum(power.reshape(CHUNK // 8, 8, BLOCK), axis=0)
                weights[odd, rows, :] = power.astype(BF)
            total = jnp.sum(total, axis=0, keepdims=True)
            base = pl.multiple_of(index * 2 * HEAD, 16)
            value = turned[pl.ds(pl.multiple_of(base + 64 * odd, 16), 80), :]
            part = dot_plain(value, weights[odd]) * (1.0 / total)
            mixed[pl.ds(pl.multiple_of(base + HEAD * odd, 8), HEAD), :] = part[8 * odd : 8 * odd + HEAD]
            peak_ref[pl.ds(head, 1), :] = peak + jnp.log2(total)
        return carry

    lax.fori_loop(0, HEADS // 2, pair, 0)
    out_ref[...] = mixed[...].T.astype(BF)


def backward_kernel(edge, *refs):
    if edge:
        (query_ref, out_ref, grad_ref, peak_ref, pair_ref, key_mark_ref, query_mark_ref,
         grad_query_ref, rim_low_ref, rim_high_ref, grad_own_ref,
         bias, turned, weights, signals, mixed, delta, view, total) = refs
    else:
        (query_ref, out_ref, grad_ref, peak_ref, pair_ref, key_mark_ref, query_mark_ref, edge_ref, _,
         grad_query_ref, grad_own_ref,
         bias, turned, weights, signals, mixed, delta, view, sem) = refs
    width = query_ref.shape[1]
    step = pl.program_id(0)
    last = (pair_ref.shape[0] - 2 * MAXLEN) // BLOCK - 1
    fill_window(step * last if edge else step + 1, last, pair_ref, view)
    inner = SPAN - MAXLEN
    if edge:
        total[...] = jnp.zeros_like(total)
        sums = total
    else:
        rows = grad_own_ref.shape[0]

        @pl.when(step == 0)
        def _():
            low = pltpu.make_async_copy(edge_ref.at[0], grad_own_ref.at[pl.ds(0, inner)], sem.at[0])
            high = pltpu.make_async_copy(
                edge_ref.at[1], grad_own_ref.at[pl.ds(rows - inner, inner)], sem.at[1]
            )
            low.start()
            high.start()
            grad_own_ref[inner : rows - inner, :] = jnp.zeros((rows - 2 * inner, 2 * width), F32)
            low.wait()
            high.wait()

        sums = grad_own_ref.at[pl.ds(pl.multiple_of(step * BLOCK + BLOCK - MAXLEN, 64), SPAN)]
    fill_mask(key_mark_ref, query_mark_ref, bias)
    turned[...] = view[:, 0:width].T
    product = out_ref[...].astype(F32) * grad_ref[...].astype(F32)
    high = product.astype(BF)
    low = (product - high.astype(F32)).astype(BF)
    of_head = (
        lax.broadcasted_iota(jnp.int32, (HEADS, width), 1) // HEAD
        == lax.broadcasted_iota(jnp.int32, (HEADS, width), 0)
    ).astype(BF)
    delta[...] = dot_rows(of_head, high) + dot_rows(of_head, low)
    factor = SCORE_SCALE * LOG2E

    def pair(index, carry):
        for odd in range(2):
            head = 2 * index + odd
            first, inside = head_lanes(head, width)
            query = masked(query_ref, first, inside)
            grad = masked(grad_ref, first, inside)
            peak = peak_ref[pl.ds(head, 1), :]
            mean = delta[pl.ds(head, 1), :]
            for start in range(0, SPAN, STRIP_BACK):
                rows = slice(start, start + STRIP_BACK)
                score = dot_rows(view[rows, pl.ds(first, 256)], query) * factor
                power = jnp.exp2(score + (bias[rows, :] - peak))
                slope = dot_rows(view[rows, pl.ds(first + width, 256)], grad)
                low = power.astype(BF)
                signal = (power * (slope - mean)).astype(BF)
                signals[odd, rows, :] = signal
                sums[rows, pl.ds(first, 256)] += dot_plain(signal, query)
                sums[rows, pl.ds(first + width, 256)] += dot_plain(low, grad)
            base = pl.multiple_of(index * 2 * HEAD, 16)
            key = turned[pl.ds(pl.multiple_of(base + 64 * odd, 16), 80), :]
            part = dot_plain(key, signals[odd]) * SCORE_SCALE
            mixed[pl.ds(pl.multiple_of(base + HEAD * odd, 8), HEAD), :] = part[8 * odd : 8 * odd + HEAD]
        return carry

    lax.fori_loop(0, HEADS // 2, pair, 0)
    grad_query_ref[...] = mixed[...].T.astype(BF)
    if edge:

        @pl.when(step == 0)
        def _():
            rim_low_ref[:, :width] = (total[0:MAXLEN, :width] * SCORE_SCALE).astype(BF)
            rim_low_ref[:, width:] = total[0:MAXLEN, width:].astype(BF)
            grad_own_ref[0] = total[MAXLEN:SPAN, :]

        @pl.when(step == 1)
        def _():
            rim_high_ref[:, :width] = (total[inner:SPAN, :width] * SCORE_SCALE).astype(BF)
            rim_high_ref[:, width:] = total[inner:SPAN, width:].astype(BF)
            grad_own_ref[0] = total[0:inner, :]
    else:

        @pl.when(step == pl.num_programs(0) - 1)
        def _():
            grad_own_ref[:, :width] = grad_own_ref[:, :width] * SCORE_SCALE


def mark_windows(marker, marker_prev, marker_next):
    wide = jnp.concatenate([marker_prev, marker, marker_next])
    count = marker.shape[0] // BLOCK
    keys = jnp.stack([wide[i * BLOCK : i * BLOCK + SPAN] for i in range(count)])[:, None, :]
    return keys, marker.reshape(count, 1, BLOCK)


def whole(shape):
    return pl.BlockSpec(shape, lambda i: (0,) * len(shape))


def attention_calls(rows, width):
    count = rows // BLOCK
    last = count - 1
    inner = SPAN - MAXLEN
    scratch = [
        pltpu.VMEM((SPAN, BLOCK), F32),
        pltpu.VMEM((width, SPAN), BF),
    ]
    elements = SPAN * BLOCK * HEADS

    def block_specs(at):
        row_block = pl.BlockSpec((BLOCK, width), lambda i: (at(i), 0))
        lane_block = pl.BlockSpec((HEADS, BLOCK), lambda i: (0, at(i)))
        key_mark = pl.BlockSpec((1, 1, SPAN), lambda i: (at(i), 0, 0))
        query_mark = pl.BlockSpec((1, 1, BLOCK), lambda i: (at(i), 0, 0))
        return row_block, lane_block, key_mark, query_mark

    any_spec = pl.BlockSpec(memory_space=pl.ANY)
    params = pltpu.CompilerParams(vmem_limit_bytes=VMEM, dimension_semantics=("arbitrary",))
    pairs = once((rows + 2 * MAXLEN, 2 * width))
    view = pltpu.VMEM((SPAN, 2 * width), BF)

    def forward(queries, key_value, marks, after):
        row_block, lane_block, key_mark, query_mark = block_specs(lambda i: i)
        return pl.pallas_call(
            skipping(forward_kernel, 4, len(after)),
            grid=(count,),
            in_specs=[row_block, pairs, key_mark, query_mark] + [any_spec] * len(after),
            out_specs=[row_block, lane_block],
            out_shape=[
                jax.ShapeDtypeStruct((rows, width), BF),
                jax.ShapeDtypeStruct((HEADS, rows), F32),
            ],
            scratch_shapes=scratch
            + [
                pltpu.VMEM((2, SPAN, BLOCK), F32),
                pltpu.VMEM((2, SPAN, BLOCK), BF),
                pltpu.VMEM((width, BLOCK), F32),
                view,
            ],
            compiler_params=params,
            cost_estimate=cost(11.5 * count),
            name="attend",
        )(queries, key_value, *marks, *after)

    def backward(edge, queries, mixed, grad, peaks, key_value, marks, before=(), after=()):
        row_block, lane_block, key_mark, query_mark = block_specs(
            (lambda i: i * last) if edge else (lambda i: i + 1)
        )
        steps = 2 if edge else count - 2
        in_specs = [row_block, row_block, row_block, lane_block, pairs]
        in_specs += [key_mark, query_mark] + [any_spec] * (len(before) + len(after))
        rim = jax.ShapeDtypeStruct((MAXLEN, 2 * width), BF)
        if edge:
            out_specs = [row_block, whole(rim.shape), whole(rim.shape),
                         pl.BlockSpec((1, inner, 2 * width), lambda i: (i, 0, 0))]
            out_shape = [jax.ShapeDtypeStruct((rows, width), BF), rim, rim,
                         jax.ShapeDtypeStruct((2, inner, 2 * width), F32)]
            extra = [view, pltpu.VMEM((SPAN, 2 * width), F32)]
        else:
            out_specs = [row_block, whole((rows, 2 * width))]
            out_shape = [jax.ShapeDtypeStruct((rows, width), BF),
                         jax.ShapeDtypeStruct((rows, 2 * width), F32)]
            extra = [view, pltpu.SemaphoreType.DMA((2,))]
        return pl.pallas_call(
            skipping(functools.partial(backward_kernel, edge), 7 + len(before), len(after)),
            grid=(steps,),
            in_specs=in_specs,
            out_specs=out_specs,
            out_shape=out_shape,
            scratch_shapes=scratch
            + [
                pltpu.VMEM((2, SPAN, BLOCK), BF),
                pltpu.VMEM((2, SPAN, BLOCK), BF),
                pltpu.VMEM((width, BLOCK), F32),
                pltpu.VMEM((HEADS, BLOCK), F32),
            ]
            + extra,
            input_output_aliases={} if edge else {8: 0},
            compiler_params=params,
            cost_estimate=cost(2.2 * steps),
            name="attend_back_edge" if edge else "attend_back_inner",
        )(queries, mixed, grad, peaks, key_value, *marks, *before, *after)

    return forward, backward


BANDS = 4
FEED_ROWS = 512
EPSILON = 1e-06
ROOT = math.sqrt(2.0 / math.pi)
CUBE = 0.044715


def skipping(kernel, first, count):
    return lambda *refs: kernel(*refs[:first], *refs[first + count :])


def once(shape):
    return pl.BlockSpec(shape, lambda i, *_: (0,) * len(shape), pipeline_mode=pl.Buffered(buffer_count=1))


def rows_of(rows, width):
    return pl.BlockSpec((rows, width), lambda i, *_: (i, 0))


def kernel_params():
    return pltpu.CompilerParams(vmem_limit_bytes=VMEM, dimension_semantics=("arbitrary",))


def cost(microseconds):
    return pl.CostEstimate(flops=int(microseconds * 1.1e9), bytes_accessed=int(microseconds * 3e6), transcendentals=0)


def dot_turned(left, right):
    return lax.dot_general(left, right, (((0,), (0,)), ((), ())), preferred_element_type=F32)


def spread(select, parts_ref, part, width):
    return dot_plain(select, parts_ref[:, part * width : (part + 1) * width])


def normalise(block):
    centred = block - jnp.mean(block, axis=-1, keepdims=True)
    inverse = lax.rsqrt(jnp.mean(centred * centred, axis=-1, keepdims=True) + EPSILON)
    return centred * inverse, inverse


def norm_back(upstream, normed, inverse):
    return inverse * (
        upstream
        - jnp.mean(upstream, axis=-1, keepdims=True)
        - normed * jnp.mean(upstream * normed, axis=-1, keepdims=True)
    )


def image_sum(gather, block):
    high = block.astype(BF)
    low = (block - high.astype(F32)).astype(BF)
    return dot_plain(gather, high) + dot_plain(gather, low)


def column_sum(block):
    rows, width = block.shape
    return jnp.sum(block.reshape(rows // 8, 8, width), axis=0)


def piece_copies(place_ref, piece_refs, full, sems):
    copies = []
    for index, piece in enumerate(piece_refs):
        rows = piece.shape[0]
        start = pl.multiple_of(place_ref[index] * 16, 16)
        copies.append(pltpu.make_async_copy(piece, full.at[pl.ds(start, rows)], sems.at[index]))
    return copies


def begin_pieces(place_ref, piece_refs, full, sems):
    @pl.when(pl.program_id(0) == 0)
    def _():
        for copy in piece_copies(place_ref, piece_refs, full, sems):
            copy.start()


def end_pieces(place_ref, piece_refs, full, sems):
    @pl.when(pl.program_id(0) == 0)
    def _():
        for copy in piece_copies(place_ref, piece_refs, full, sems):
            copy.wait()


def project_kernel(own_rows, tokens_ref, select_ref, parts_ref, bias_ref, weight_ref, input_ref, query_ref, pair_ref):
    width = tokens_ref.shape[1]
    select = select_ref[...]
    normed, _ = normalise(tokens_ref[...].astype(F32))
    shift = spread(select, parts_ref, 0, width)
    scale = spread(select, parts_ref, 1, width)
    rows = (normed * (1.0 + scale) + shift).astype(BF)
    input_ref[...] = rows

    @pl.when(pl.program_id(0) * tokens_ref.shape[0] < own_rows)
    def _():
        query_ref[...] = (dot_plain(rows, weight_ref[:, :width]) + bias_ref[:, :width]).astype(BF)

    pair_ref[:, :width] = dot_plain(rows, weight_ref[:, width : 2 * width]).astype(BF)
    pair_ref[:, width:] = (dot_plain(rows, weight_ref[:, 2 * width :]) + bias_ref[:, width:]).astype(BF)


def project(weight, own_rows, tokens, select, parts, bias):
    rows, width = tokens.shape
    band = rows // BANDS
    return pl.pallas_call(
        functools.partial(project_kernel, own_rows),
        grid=(BANDS,),
        in_specs=[
            rows_of(band, width),
            rows_of(band, select.shape[1]),
            once(parts.shape),
            once(bias.shape),
            once(weight.shape),
        ],
        out_specs=[rows_of(band, width), rows_of(band, width), rows_of(band, 2 * width)],
        out_shape=[
            jax.ShapeDtypeStruct((rows, width), BF),
            jax.ShapeDtypeStruct((rows, width), BF),
            jax.ShapeDtypeStruct((rows, 2 * width), BF),
        ],
        compiler_params=kernel_params(),
        cost_estimate=cost(25),
        name="project",
    )(tokens, select, parts, bias, weight)


def enter_feed_kernel(count, place_ref, mixed_ref, tokens_ref, cotangent_ref, select_ref, parts_ref, bias_ref, *refs):
    pieces = refs[:count]
    attn_ref, middle_ref, input_ref, grad_feed_ref, full, sems = refs[count:]
    width = tokens_ref.shape[1]
    begin_pieces(place_ref, pieces, full, sems)
    select = select_ref[...]
    gate_mixer = spread(select, parts_ref, 0, width)
    shift = spread(select, parts_ref, 1, width)
    scale = spread(select, parts_ref, 2, width)
    gate_feed = spread(select, parts_ref, 3, width)
    grad_feed_ref[...] = (cotangent_ref[...].astype(F32) * gate_feed).astype(BF)
    end_pieces(place_ref, pieces, full, sems)
    attn = dot_plain(mixed_ref[...], full[...]) + bias_ref[...]
    attn_ref[...] = attn
    middle = tokens_ref[...].astype(F32) + gate_mixer * attn
    middle_ref[...] = middle
    normed, _ = normalise(middle)
    input_ref[...] = (normed * (1.0 + scale) + shift).astype(BF)


def enter_feed(place, pieces, mixed, tokens, cotangent, select, parts, bias, after):
    rows, width = tokens.shape
    band = rows // BANDS
    any_spec = pl.BlockSpec(memory_space=pl.ANY)
    block = rows_of(band, width)
    return pl.pallas_call(
        skipping(functools.partial(enter_feed_kernel, len(pieces)), 7 + len(pieces), len(after)),
        grid_spec=pltpu.PrefetchScalarGridSpec(
            num_scalar_prefetch=1,
            grid=(BANDS,),
            in_specs=[block, block, block, rows_of(band, select.shape[1]), once(parts.shape), once(bias.shape)]
            + [any_spec] * (len(pieces) + len(after)),
            out_specs=[block] * 4,
            scratch_shapes=[pltpu.VMEM((width, width), BF), pltpu.SemaphoreType.DMA((len(pieces),))],
        ),
        out_shape=[jax.ShapeDtypeStruct((rows, width), kind) for kind in (F32, F32, BF, BF)],
        compiler_params=kernel_params(),
        cost_estimate=cost(14),
        name="enter_feed",
    )(place, mixed, tokens, cotangent, select, parts, bias, *pieces, *after)


def feed_kernel(later, place_ref, input_ref, grad_ref, expand_ref, bias_ref, *refs):
    if later:
        contract_ref, before_out_ref, before_grad_ref = refs[:3]
        refs = refs[7:]
    else:
        own_ref, near_ref = refs[:2]
        held, sems = refs[-2:]
        refs = refs[2:-2]
        before_out_ref = before_grad_ref = None
        step = pl.program_id(0)
        own_copy = pltpu.make_async_copy(own_ref, held.at[0], sems.at[0])
        near_copy = pltpu.make_async_copy(near_ref, held.at[1], sems.at[1])

        @pl.when(step == 0)
        def _():
            own_copy.start()
            near_copy.start()
            own_copy.wait()

        @pl.when(step == 1)
        def _():
            near_copy.wait()

        contract_ref = held.at[step]
    feed_step(place_ref, input_ref, grad_ref, expand_ref, contract_ref, bias_ref, before_out_ref, before_grad_ref, *refs)


def feed_step(place_ref, input_ref, grad_ref, expand_ref, contract_ref, bias_ref, before_out_ref, before_grad_ref,
                out_ref, grad_input_ref, keep_ref, send_ref, contract_grad_ref, bias_grad_ref, grad_sum_ref,
                input_turned, grad_turned, active, hidden_grad):
    step = pl.program_id(0)
    rows, width = input_ref.shape

    @pl.when(step == 0)
    def _():
        input_turned[...] = input_ref[...].T
        grad_turned[...] = grad_ref[...].T
        grad_sum_ref[...] = column_sum(grad_ref[...].astype(F32))
        if before_out_ref is None:
            out_ref[...] = jnp.zeros_like(out_ref)
            grad_input_ref[...] = jnp.zeros_like(grad_input_ref)
        else:
            out_ref[...] = before_out_ref[...]
            grad_input_ref[...] = before_grad_ref[...]

    bias_grad_ref[...] = jnp.zeros_like(bias_grad_ref)

    def band(index, carry):
        here = pl.ds(pl.multiple_of(index * FEED_ROWS, FEED_ROWS), FEED_ROWS)
        hidden = dot_plain(input_ref[here, :], expand_ref[...]) + bias_ref[...]
        square = hidden * hidden
        bent = jnp.tanh(ROOT * hidden * (1.0 + CUBE * square))
        half = 0.5 + 0.5 * bent
        active[here, :] = (hidden * half).astype(BF)
        slope = half + (0.5 * ROOT) * hidden * (1.0 - bent * bent) * (1.0 + (3.0 * CUBE) * square)
        pulled = dot_rows(grad_ref[here, :], contract_ref[...])
        low = (pulled * slope).astype(BF)
        hidden_grad[here, :] = low
        bias_grad_ref[...] += column_sum(low.astype(F32))
        out_ref[here, :] += dot_plain(active[here, :], contract_ref[...])
        grad_input_ref[here, :] += dot_rows(low, expand_ref[...])
        return carry

    lax.fori_loop(0, rows // FEED_ROWS, band, 0)
    share = width // 4
    block = keep_ref.shape[4]
    for index in range(4):
        start = pl.multiple_of(place_ref[index] * 16, 16)
        part = dot_plain(input_turned[pl.ds(start, share), :], hidden_grad[...]).astype(BF)
        store_owners(send_ref if index % 2 else keep_ref, place_ref[4 + index], part, 0, block, 0)
    for index in range(4):
        here = slice(index * share, (index + 1) * share)
        part = dot_plain(grad_turned[here, :], active[...]).astype(BF)
        if len(contract_grad_ref.shape) == 3:
            contract_grad_ref[0, here, :] = part
        else:
            rows = contract_grad_ref.shape[3]
            for start in range(0, share, rows):
                rest, side = divmod((index * share + start) // rows, 2)
                contract_grad_ref[0, side, rest] = part[start : start + rows]


def feed(place, seq_count, inputs, grad_feed, expand, contracts, bias, before=()):
    rows, width = inputs.shape
    hidden = expand.shape[1]
    quarters = hidden // width
    whole_rows = once((rows, width))
    rest = seq_count // 2
    expand_shape = (2, 2, rest, width // 4, hidden // seq_count)
    expand_block = pl.BlockSpec((2, 2, rest // quarters) + expand_shape[3:], lambda i, place: (0, 0, place[8 + i], 0, 0))
    if width // seq_count % 16 == 0:
        contract_shape = (quarters, 2, rest, width // seq_count, width)
    else:
        contract_shape = (quarters, width, width)
    zeros = (0,) * (len(contract_shape) - 1)
    any_spec = pl.BlockSpec(memory_space=pl.ANY)
    result = pl.pallas_call(
        functools.partial(feed_kernel, bool(before)),
        grid_spec=pltpu.PrefetchScalarGridSpec(
            num_scalar_prefetch=1,
            grid=(quarters // 2,),
            in_specs=[
                whole_rows,
                whole_rows,
                pl.BlockSpec((width, width), lambda i, place: (0, place[8 + i])),
                pl.BlockSpec((1, width), lambda i, place: (0, place[8 + i])),
            ]
            + (
                [pl.BlockSpec((width, width), lambda i, place: (place[8 + i], 0))] + [whole_rows] * 2 + [any_spec] * 4
                if before
                else [any_spec] * 2
            ),
            out_specs=[
                whole_rows,
                whole_rows,
                expand_block,
                expand_block,
                pl.BlockSpec((1,) + contract_shape[1:], lambda i, place: (place[8 + i],) + zeros),
                pl.BlockSpec((8, width), lambda i, place: (0, place[8 + i])),
                once((8, width)),
            ],
            scratch_shapes=[
                pltpu.VMEM((width, rows), BF),
                pltpu.VMEM((width, rows), BF),
                pltpu.VMEM((rows, width), BF),
                pltpu.VMEM((rows, width), BF),
            ]
            + ([] if before else [pltpu.VMEM((2, width, width), BF), pltpu.SemaphoreType.DMA((2,))]),
        ),
        out_shape=[
            jax.ShapeDtypeStruct((rows, width), F32),
            jax.ShapeDtypeStruct((rows, width), F32),
            jax.ShapeDtypeStruct(expand_shape, BF),
            jax.ShapeDtypeStruct(expand_shape, BF),
            jax.ShapeDtypeStruct(contract_shape, BF),
            jax.ShapeDtypeStruct((8, hidden), F32),
            jax.ShapeDtypeStruct((8, width), F32),
        ],
        input_output_aliases={8: 2, 9: 3, 10: 4, 11: 5} if before else {},
        compiler_params=kernel_params(),
        cost_estimate=cost(47),
        name="feed_later" if before else "feed",
    )(place, inputs, grad_feed, expand, bias, *contracts, *before)
    return result


def leave_feed_kernel(count, place_ref, feed_ref, grad_input_ref, middle_ref, attn_ref, cotangent_ref, select_ref,
                      gather_ref, parts_ref, bias_ref, *refs):
    pieces = refs[:count]
    out_ref, grad_middle_ref, grad_attn_ref, grad_mixed_ref, image_ref, sum_ref, full, sems = refs[count:]
    width = middle_ref.shape[1]
    step = pl.program_id(0)
    begin_pieces(place_ref, pieces, full, sems)
    select = select_ref[...]
    gather = gather_ref[...]

    @pl.when(step == 0)
    def _():
        image_ref[...] = jnp.zeros_like(image_ref)
        sum_ref[...] = jnp.zeros_like(sum_ref)

    middle = middle_ref[...]
    grad_out = cotangent_ref[...].astype(F32)
    feed_out = feed_ref[...] + bias_ref[...]
    out_ref[...] = (middle + spread(select, parts_ref, 3, width) * feed_out).astype(BF)
    image_ref[:, 3 * width :] += image_sum(gather, grad_out * feed_out)
    grad_input = grad_input_ref[...]
    image_ref[:, width : 2 * width] += image_sum(gather, grad_input)
    normed, inverse = normalise(middle)
    image_ref[:, 2 * width : 3 * width] += image_sum(gather, grad_input * normed)
    scale = spread(select, parts_ref, 2, width)
    grad_middle = grad_out + norm_back(grad_input * (1.0 + scale), normed, inverse)
    grad_middle_ref[...] = grad_middle
    image_ref[:, :width] += image_sum(gather, grad_middle * attn_ref[...])
    grad_attn = (grad_middle * spread(select, parts_ref, 0, width)).astype(BF)
    grad_attn_ref[...] = grad_attn
    sum_ref[...] += column_sum(grad_attn.astype(F32))
    end_pieces(place_ref, pieces, full, sems)
    grad_mixed_ref[...] = dot_rows(grad_attn, full[...]).astype(BF)


def leave_feed(place, pieces, feed_out, grad_input, middle, attn, cotangent, select, gather, parts, bias, after):
    rows, width = middle.shape
    band = rows // BANDS
    any_spec = pl.BlockSpec(memory_space=pl.ANY)
    block = rows_of(band, width)
    images = gather.shape[0]
    return pl.pallas_call(
        skipping(functools.partial(leave_feed_kernel, len(pieces)), 10 + len(pieces), len(after)),
        grid_spec=pltpu.PrefetchScalarGridSpec(
            num_scalar_prefetch=1,
            grid=(BANDS,),
            in_specs=[block] * 5
            + [rows_of(band, select.shape[1]), pl.BlockSpec((images, band), lambda i, *_: (0, i)),
               once(parts.shape), once(bias.shape)]
            + [any_spec] * (len(pieces) + len(after)),
            out_specs=[block] * 4 + [once((images, 4 * width)), once((8, width))],
            scratch_shapes=[pltpu.VMEM((width, width), BF), pltpu.SemaphoreType.DMA((len(pieces),))],
        ),
        out_shape=[jax.ShapeDtypeStruct((rows, width), kind) for kind in (BF, F32, BF, BF)]
        + [jax.ShapeDtypeStruct((images, 4 * width), F32), jax.ShapeDtypeStruct((8, width), F32)],
        compiler_params=kernel_params(),
        cost_estimate=cost(2.2),
        name="leave_feed",
    )(place, feed_out, grad_input, middle, attn, cotangent, select, gather, parts, bias, *pieces, *after)


def store_owners(out_ref, lead, part, first, block, base):
    columns = part.shape[1]
    at = 0
    while at < columns:
        owner, offset = divmod(first + at, block)
        count = min(block - offset, columns - at)
        rest, side = divmod(owner, 2)
        out_ref[lead, side, rest, :, base + offset : base + offset + count] = part[:, at : at + count]
        at += count


def weight_grad_kernel(place_ref, input_ref, query_ref, pair_ref, mixed_ref, attn_ref, keep_ref, send_ref, turned):
    step = pl.program_id(0)
    width = query_ref.shape[1]
    share = width // 4
    block = keep_ref.shape[4] // 4

    def store(grad_ref, first, block, base):
        for index in range(4):
            start = pl.multiple_of(place_ref[index] * 16, 16)
            part = dot_plain(turned[pl.ds(start, share), :], grad_ref[...]).astype(BF)
            store_owners(send_ref if index % 2 else keep_ref, place_ref[4 + index], part, first, block, base)

    @pl.when(step == 0)
    def _():
        turned[...] = input_ref[...].T
        store(query_ref, 0, 3 * block, 0)

    for number in (1, 2):

        @pl.when(step == number)
        def _(number=number):
            store(pair_ref, number * width, 3 * block, 0)

    @pl.when(step == 3)
    def _():
        turned[...] = mixed_ref[...].T
        store(attn_ref, 0, block, 3 * block)


def weight_grad(place, seq_count, inputs, query, pair, mixed, attn, after):
    rows, width = query.shape
    shape = (2, 2, seq_count // 2, width // 4, 4 * width // seq_count)
    whole_rows = once((rows, width))
    return pl.pallas_call(
        skipping(weight_grad_kernel, 6, len(after)),
        grid_spec=pltpu.PrefetchScalarGridSpec(
        num_scalar_prefetch=1,
        grid=(4,),
        in_specs=[
            whole_rows,
            whole_rows,
            pl.BlockSpec((rows, width), lambda i, *_: (0, jnp.clip(i - 1, 0, 1))),
            whole_rows,
            whole_rows,
        ]
        + [pl.BlockSpec(memory_space=pl.ANY)] * len(after),
        out_specs=[once(shape), once(shape)],
        scratch_shapes=[pltpu.VMEM((width, rows), BF)],
        ),
        out_shape=[jax.ShapeDtypeStruct(shape, BF)] * 2,
        compiler_params=kernel_params(),
        cost_estimate=cost(2),
        name="weight_grad",
    )(place, inputs, query, pair, mixed, attn, *after)


def leave_kernel(query_ref, pair_ref, tokens_ref, grad_middle_ref, select_ref, gather_ref, parts_ref, weight_ref,
                 feed_images_ref, grad_ref, image_ref, sum_ref):
    width = tokens_ref.shape[1]
    select = select_ref[...]
    gather = gather_ref[...]

    @pl.when(pl.program_id(0) == 0)
    def _():
        image_ref[:, : 2 * width] = jnp.zeros_like(image_ref[:, : 2 * width])
        image_ref[:, 2 * width :] = feed_images_ref[...]
        sum_ref[...] = jnp.zeros_like(sum_ref)

    query = query_ref[...]
    pair = pair_ref[...]
    sum_ref[:, :width] += column_sum(query.astype(F32))
    sum_ref[:, width:] += column_sum(pair[:, width:].astype(F32))
    normed, inverse = normalise(tokens_ref[...].astype(F32))
    scale = spread(select, parts_ref, 1, width)
    grad_input = dot_rows(query, weight_ref[:, :width]) + dot_rows(pair, weight_ref[:, width:])
    image_ref[:, :width] += image_sum(gather, grad_input)
    image_ref[:, width : 2 * width] += image_sum(gather, grad_input * normed)
    grad_ref[...] = grad_middle_ref[...] + norm_back(grad_input * (1.0 + scale), normed, inverse)


def leave(weight, query, pair, tokens, grad_middle, select, gather, parts, feed_images, after):
    rows, width = tokens.shape
    band = rows // BANDS
    block = rows_of(band, width)
    images = gather.shape[0]
    return pl.pallas_call(
        skipping(leave_kernel, 9, len(after)),
        grid=(BANDS,),
        in_specs=[block, rows_of(band, 2 * width), block, block, rows_of(band, select.shape[1]),
                  pl.BlockSpec((images, band), lambda i: (0, i)), once(parts.shape), once(weight.shape),
                  once(feed_images.shape)]
        + [pl.BlockSpec(memory_space=pl.ANY)] * len(after),
        out_specs=[block, once((images, 6 * width)), once((8, 2 * width))],
        out_shape=[
            jax.ShapeDtypeStruct((rows, width), F32),
            jax.ShapeDtypeStruct((images, 6 * width), F32),
            jax.ShapeDtypeStruct((8, 2 * width), F32),
        ],
        compiler_params=kernel_params(),
        cost_estimate=cost(2.5),
        name="leave",
    )(query, pair, tokens, grad_middle, select, gather, parts, weight, feed_images, *after)


def partners(axis, bit):
    return [(i, i ^ bit) for i in range(lax.axis_size(axis))]


def bits_of(axis):
    bit = 1
    while bit < lax.axis_size(axis):
        yield bit
        bit *= 2


def doubled(value, axis, bits=None):
    place = lax.axis_index(axis)
    for bit in bits_of(axis) if bits is None else bits:
        other = lax.ppermute(value, axis, partners(axis, bit))
        mine = (place // bit) % 2
        value = jnp.concatenate([jnp.where(mine == 0, value, other), jnp.where(mine == 0, other, value)])
    return value


def neighbour_groups():
    dp_count, seq_count = lax.axis_size("dp"), lax.axis_size("seq")
    return [
        [d * seq_count + 2 * pair + side for d in range(dp_count) for side in range(2)]
        for pair in range(seq_count // 2)
    ]


def gathered(weight):
    rows = weight.shape[0] // 2
    half = lax.dynamic_slice_in_dim(weight, lax.axis_index("seq") % 2 * rows, rows, 0)
    return lax.all_gather(half, ("dp", "seq"), axis=0, tiled=True, axis_index_groups=neighbour_groups())


def scattered(grad):
    return lax.psum_scatter(
        grad.reshape(-1, *grad.shape[2:]), ("dp", "seq"), scatter_dimension=0, axis_index_groups=neighbour_groups()
    )


def scattered_core(keep, send, other):
    seq_count = lax.axis_size("seq")
    total = gate((wide(keep) + wide(swapped(send, "dp", 1))).astype(BF), other)
    groups = [
        [(2 * y + core) * seq_count + 2 * pair + side for y in range(2) for side in range(2)]
        for core in range(2)
        for pair in range(seq_count // 2)
    ]
    return total, lax.psum_scatter(
        total.reshape(-1, *total.shape[2:]), ("dp", "seq"), scatter_dimension=0, axis_index_groups=groups
    )


def along_rest(rest):
    stages = []
    for bit in list(bits_of("seq"))[1:]:
        pairs = rest.reshape(-1, 2, *rest.shape[1:])
        mine = (lax.axis_index("seq") // bit) % 2
        sent = lax.dynamic_index_in_dim(pairs, 1 - mine, 1, keepdims=False)
        rest = wide(lax.dynamic_index_in_dim(pairs, mine, 1, keepdims=False)) + wide(swapped(sent, "seq", bit))
        stages.append(rest)
    return stages


def gate(value, other):
    first = other[(0,) * other.ndim]
    return jnp.where(first == first, value, jnp.zeros_like(value))


def swapped(value, axis, bit, kind=BF):
    return lax.ppermute(value.astype(kind), axis, partners(axis, bit))


def wide(value):
    return value.astype(F32)


def split_owners(value):
    return value.reshape(2, -1, 2, *value.shape[2:])


def three_terms(value):
    high = lax.reduce_precision(value, 8, 7)
    middle = lax.reduce_precision(value - high, 8, 7)
    low = value - high - middle
    high, middle, low = high.astype(BF), middle.astype(BF), low.astype(BF)
    pad = jnp.zeros((TERMS - 3 * WIN, value.shape[1]), BF)
    return jnp.concatenate([high, middle, low, pad])


def shards(
    tokens,
    segments,
    condition,
    cotangent,
    modulation_weight,
    modulation_bias,
    input_weight,
    query_value_bias,
    output_weight,
    output_bias,
    expand_weight,
    expand_bias,
    contract_weight,
    contract_bias,
):
    token_rows = tokens[0]
    segment = segments[0]
    conditions = condition[0].astype(F32)
    grad_out = cotangent[0]
    row_count, width = token_rows.shape
    images = conditions.shape[0]
    own = lax.axis_index("dp")
    place_in_seq = lax.axis_index("seq")
    seq_count = lax.axis_size("seq")
    onward = [(i, i + 1) for i in range(seq_count - 1)]
    back = [(i + 1, i) for i in range(seq_count - 1)]
    columns = modulation_weight.shape[1] // seq_count
    row = lambda bias: bias.astype(F32)[None, :]

    input_full = gathered(input_weight)
    expand_full = gathered(expand_weight)
    contract_full = gathered(contract_weight)
    silu_all, silu_back = jax.vjp(jax.nn.silu, conditions)
    cond_act = silu_all.astype(BF)
    late = 2 * width
    mixer_columns = late // seq_count
    feed_columns = 4 * width // seq_count
    share_rows = width // 4
    seq_bits, dp_bits = list(bits_of("seq")), list(bits_of("dp"))

    def own_columns(array, axis):
        return jnp.concatenate(
            [
                lax.dynamic_slice_in_dim(array, place_in_seq * mixer_columns, mixer_columns, axis),
                lax.dynamic_slice_in_dim(array, late + place_in_seq * feed_columns, feed_columns, axis),
            ],
            axis=axis,
        )

    first_image = jnp.clip(segment[0] - BEFORE, 0, images - WIN)
    top = seq_bits[-1]
    first_of_top = lax.ppermute(first_image, "seq", partners("seq", top))
    marker = segment + 1
    low_marks = lax.ppermute(jnp.append(marker[row_count - MAXLEN :], first_image), "seq", onward)
    high_marks = lax.ppermute(jnp.append(marker[:MAXLEN], first_image), "seq", back)
    low_rows = lax.ppermute(token_rows[row_count - MAXLEN :], "seq", onward)
    high_rows = lax.ppermute(token_rows[:MAXLEN], "seq", back)
    first_of_next = jnp.where(place_in_seq % 2 == 0, high_marks[MAXLEN], low_marks[MAXLEN])
    piece = own_columns(modulation_weight, 1)
    piece_far = lax.ppermute(piece, "dp", partners("dp", 2))
    piece = jnp.concatenate([piece, piece_far])
    piece = jnp.concatenate([piece, lax.ppermute(piece, "dp", partners("dp", 1))])
    turned = [lax.dynamic_slice_in_dim(cond_act, (own ^ index) * share_rows, share_rows, 1) for index in (0, 2, 1, 3)]
    product = jnp.dot(jnp.concatenate(turned, axis=1), piece, preferred_element_type=F32)
    product += row(own_columns(modulation_bias, 0))
    product = doubled(product[None], "seq", seq_bits[:1])
    output_far = lax.ppermute(gate(output_weight, product), "dp", partners("dp", 2))
    product = doubled(product, "seq", seq_bits[1:-1])
    for early in (low_rows, high_rows, first_of_next.astype(F32)[None], first_of_top.astype(F32)[None]):
        product = gate(product, early)
    mine = lax.dynamic_slice_in_dim(product, first_image, WIN, 1)
    other = lax.ppermute(lax.dynamic_slice_in_dim(product, first_of_top, WIN, 1), "seq", partners("seq", top))
    upper = place_in_seq // top
    windows = jnp.concatenate([jnp.where(upper == 0, mine, other), jnp.where(upper == 0, other, mine)])
    mixer_parts = three_terms(windows[:, :, :mixer_columns].swapaxes(0, 1).reshape(WIN, -1))
    feed_parts = three_terms(windows[:, :, mixer_columns:].swapaxes(0, 1).reshape(WIN, -1))
    marks = mark_windows(marker, low_marks[:MAXLEN], high_marks[:MAXLEN])
    wide_rows = jnp.concatenate([token_rows, low_rows, high_rows])
    wide_segment = jnp.concatenate([segment, low_marks[:MAXLEN] - 1, high_marks[:MAXLEN] - 1])
    image_select = (wide_segment - first_image)[:, None] == jnp.arange(WIN, dtype=jnp.int32)[None, :]
    select = jnp.concatenate(
        [image_select, image_select, image_select, jnp.zeros((wide_segment.shape[0], TERMS - 3 * WIN), bool)], axis=1
    ).astype(BF)
    gather = jnp.concatenate(
        [image_select[:row_count].T, jnp.zeros((WIN_PAD - WIN, row_count), bool)], axis=0
    ).astype(BF)

    input_attn, queries, key_value = project(
        input_full, row_count, wide_rows, select, mixer_parts, row(query_value_bias)
    )
    output_near = lax.ppermute(output_weight, "dp", partners("dp", 1))
    output_pieces = [output_weight, output_near, output_far, lax.ppermute(output_far, "dp", partners("dp", 1))]
    output_at = (jnp.stack([own ^ index for index in range(4)]) * (share_rows // 16)).astype(jnp.int32)
    acts = [cond_act] + [lax.ppermute(gate(cond_act, input_attn), "dp", partners("dp", mask)) for mask in (1, 2, 3)]
    own_slice = lax.dynamic_slice_in_dim(modulation_weight, place_in_seq * columns, columns, 1)
    slice_full = lax.all_gather(own_slice, "dp", axis=0, tiled=True)

    attend, attend_back = attention_calls(row_count, width)
    attn_mixed, row_peaks = attend(queries, key_value, marks, ())

    attn_out, middle, input_feed, grad_feed = enter_feed(
        output_at, output_pieces, attn_mixed, token_rows, grad_out, select, feed_parts, row(output_bias),
        (),
    )
    chunks = jnp.stack([own ^ index for index in range(4)])
    chunks = jnp.concatenate([chunks * (share_rows // 16), chunks // 2, chunks]).astype(jnp.int32)
    contract_pair = contract_weight, lax.ppermute(contract_weight, "dp", partners("dp", 1))
    feed_before = feed(chunks[:10], seq_count, input_feed, grad_feed, expand_full, contract_pair, row(expand_bias))
    later = jnp.concatenate([chunks[:8], chunks[10:]])
    feed_out, grad_input_feed, expand_keep, expand_send, contract_grad, expand_sums, feed_sums = feed(
        later, seq_count, input_feed, grad_feed, expand_full, (contract_full,), row(expand_bias), feed_before[:6]
    )
    if len(contract_grad.shape) == 3:
        contract_grad = contract_grad.reshape(4, seq_count // 2, 2, width // seq_count, width).swapaxes(1, 2)
    contract_rest = scattered(contract_grad)
    layer_out, grad_middle, grad_attn, grad_mixed, feed_images, attn_sums = leave_feed(
        output_at, output_pieces, feed_out, grad_input_feed, middle, attn_out, grad_out, select, gather,
        feed_parts, row(contract_bias), (*acts[1:], slice_full),
    )
    expand_total, expand_rest = scattered_core(expand_keep, expand_send, grad_mixed)
    grad_query_edge, rim_low, rim_high, grad_edge = attend_back(
        True, queries, attn_mixed, grad_mixed, row_peaks, key_value, marks, (), (expand_total,)
    )
    from_next = lax.ppermute(rim_low, "seq", back)
    from_prev = lax.ppermute(rim_high, "seq", onward)
    grad_query, own_grad = attend_back(
        False, queries, attn_mixed, grad_mixed, row_peaks, key_value,
        marks, (grad_edge, grad_query_edge), (contract_rest,),
    )
    rims = jnp.pad(from_prev.astype(F32), ((0, row_count - MAXLEN), (0, 0))) + jnp.pad(
        from_next.astype(F32), ((row_count - MAXLEN, 0), (0, 0))
    )
    grad_pair = (own_grad + rims).astype(BF)
    contract_stages = along_rest(contract_rest)
    total_contract = contract_stages[-1][0]
    total_expand = along_rest(expand_rest)[-1][0]
    input_keep, input_send = weight_grad(
        chunks, seq_count, input_attn, grad_query, grad_pair, attn_mixed, grad_attn, (contract_stages[0],)
    )
    input_rest = scattered_core(input_keep, input_send, input_keep)[1]
    grad_rows, all_images, packed_sums = leave(
        input_full, grad_query, grad_pair, token_rows, grad_middle, select, gather, mixer_parts, feed_images,
        (input_send,),
    )
    input_stages = along_rest(input_rest)
    input_total = input_stages[-1][0]
    input_width = 3 * width // seq_count
    total_input, total_output = input_total[:, :input_width], input_total[:, input_width:]

    window_grads = all_images[:WIN]
    sums = [
        jnp.sum(window_grads, axis=0),
        jnp.sum(packed_sums, axis=0),
        jnp.sum(attn_sums, axis=0),
        jnp.sum(expand_sums, axis=0),
        jnp.sum(feed_sums, axis=0),
    ]
    ends = [sum(part.shape[0] for part in sums[: index + 1]) for index in range(5)]
    whole_length = -(-ends[-1] // columns) * columns
    biases = sum(
        jnp.pad(part, (end - part.shape[0], whole_length - end)) for part, end in zip(sums, ends)
    ).reshape(-1, columns)
    bias_rows = biases.shape[0]

    def joined(value, axis, bit):
        high = lax.reduce_precision(biases, 8, 7)
        low = lax.reduce_precision(biases - high, 8, 7)
        got = swapped(jnp.concatenate([value.reshape(-1, columns), high, low]), axis, bit)
        rest = high + low + (wide(got[-2 * bias_rows : -bias_rows]) + wide(got[-bias_rows:]))
        return wide(got[: -2 * bias_rows]).reshape(value.shape), rest

    window_blocks = window_grads.reshape(WIN, -1, 2, columns)
    mine = lax.dynamic_index_in_dim(window_blocks, place_in_seq % 2, 2, keepdims=False)
    sent = lax.dynamic_index_in_dim(window_blocks, 1 - place_in_seq % 2, 2, keepdims=False)
    got, biases = joined(sent.swapaxes(0, 1), "seq", 1)
    empty = jnp.zeros((seq_count // 2, images, columns), F32)
    column_grads = lax.dynamic_update_slice_in_dim(empty, mine.swapaxes(0, 1), first_image, 1)
    column_grads += lax.dynamic_update_slice_in_dim(empty, got, first_of_next, 1)
    for bit in seq_bits[1:]:
        pairs = column_grads.reshape(-1, 2, images, columns)
        mine = (place_in_seq // bit) % 2
        got, biases = joined(lax.dynamic_index_in_dim(pairs, 1 - mine, 1, keepdims=False), "seq", bit)
        column_grads = lax.dynamic_index_in_dim(pairs, mine, 1, keepdims=False) + got
    column_grads = gate(column_grads[0], input_rest)
    all_grads = column_grads[None].astype(BF)
    for bit in dp_bits:
        other, biases = joined(all_grads, "dp", bit)
        other = other.astype(BF)
        mine = (own // bit) % 2
        all_grads = jnp.concatenate([jnp.where(mine == 0, all_grads, other), jnp.where(mine == 0, other, all_grads)])
    all_grads = all_grads.reshape(-1, columns)
    acts = jnp.stack([lax.dynamic_slice_in_dim(act, own * share_rows, share_rows, 1) for act in acts])
    acts = [lax.dynamic_index_in_dim(acts, own ^ index, 0, keepdims=False) for index in range(4)]
    all_act = jnp.concatenate(acts)
    total_modulation = dot_turned(all_act, all_grads)
    grad_act = lax.dot_general(
        column_grads, slice_full.astype(F32), (((1,), (1,)), ((), ())), precision=lax.Precision.HIGHEST
    )
    grad_condition = silu_back(grad_act)[0].reshape(seq_count, -1, width)
    for bit in seq_bits:
        if bit == seq_bits[1]:
            grad_condition = gate(grad_condition, input_stages[0])
        pairs = grad_condition.reshape(-1, 2, *grad_condition.shape[1:])
        mine = (place_in_seq // bit) % 2
        got = swapped(lax.dynamic_index_in_dim(pairs, 1 - mine, 1, keepdims=False), "seq", bit, F32)
        grad_condition = lax.dynamic_index_in_dim(pairs, mine, 1, keepdims=False) + got
    grad_condition = grad_condition[0]
    bias_modulation, bias_query_value, bias_output, bias_expand, bias_contract, _ = jnp.split(
        biases.reshape(-1), ends
    )
    return (
        layer_out[None],
        grad_rows[None],
        grad_condition[None],
        total_modulation,
        bias_modulation,
        total_input,
        bias_query_value,
        total_output,
        bias_output,
        total_expand,
        bias_expand,
        total_contract.T,
        bias_contract,
    )


def solution(mesh):
    in_specs = (
        P("dp", "seq", None),
        P("dp", "seq"),
        P("dp", None, None),
        P("dp", "seq", None),
        P("dp", None),
        P(),
        P("dp", None),
        P(),
        P("dp", None),
        P(),
        P("dp", None),
        P(),
        P("dp", None),
        P(),
    )
    out_specs = (
        P("dp", "seq", None),
        P("dp", "seq", None),
        P("dp", "seq", None),
        P("dp", "seq"),
        P(),
        P("dp", "seq"),
        P(),
        P("dp", "seq"),
        P(),
        P("dp", "seq"),
        P(),
        P("dp", "seq"),
        P(),
    )
    return jax.shard_map(shards, mesh=mesh, in_specs=in_specs, out_specs=out_specs, check_vma=False)
```
